256 devices in a mesh: dp: 16 (over y_lo, z), seq: 16 (over x, y_hi, core).
Axes of the slice: x: 4, y: 4 (y_hi: 2, y_lo: 2; y = y_hi * 2 + y_lo), z: 8, core: 2. Of those that a mesh axis runs over, the one named last changes fastest.
Arguments:
- seq_embed: bfloat16 [16, 3072, 1536], P('dp', 'seq'), may hold values from -24 to 24
- w_qkv: bfloat16 [1536, 2304], P('seq'), may hold values from -1 to 1
- upstream: bfloat16 [16, 3072, 768], P('dp', 'seq'), may hold values from -6 to 6
Outputs:
- attended: bfloat16 [16, 3072, 768], P('dp', 'seq')
- grad_input: bfloat16 [16, 3072, 1536], P('dp', 'seq')
- grad_qkv: bfloat16 [1536, 2304], P('seq')
The draws below stay inside these ranges and needn't reach their ends.
All inputs are finite; a program needn't handle non-finite values.
Results may differ from the reference program's by a relative error of at most 0.04.
Values may be sent and summed in bfloat16 or wider, within the bound.
A program may use at most 128 MiB of HBM per device.

```python
import math
import jax
import jax.numpy as jnp
from jax import lax

D = 1536
HEADS = 6
HD = 128
POS_DEV = 192
BATCH = 16
LENGTH = 3072
N_SEQ = 16


def draw_seq_embed(key, part):
    key = jax.random.fold_in(key, 11)
    noise_key = jax.random.fold_in(key, 0)
    base = jnp.clip(jax.random.normal(noise_key, (BATCH, LENGTH, D), jnp.float32), -6.0, 6.0)
    return base.astype(jnp.bfloat16)


def draw_w_qkv(key, part):
    key = jax.random.fold_in(key, 23)
    query_key, key_key, value_key = jax.random.split(key, 3)
    width = HEADS * HD
    spread = D ** (-0.5)
    query_part = jnp.clip(jax.random.normal(query_key, (D, width), jnp.float32), -6.0, 6.0) * spread
    key_part = jnp.clip(jax.random.normal(key_key, (D, width), jnp.float32), -6.0, 6.0) * spread
    value_part = jnp.clip(jax.random.normal(value_key, (D, width), jnp.float32), -6.0, 6.0) * spread
    return jnp.concatenate([query_part, key_part, value_part], axis=1).astype(jnp.bfloat16)


def steps_of(rng, extent, cuts, low, high):
    factor_of = 1.0
    for position, shards_of in cuts:
        steps = jax.random.uniform(jax.random.fold_in(jax.random.fold_in(rng, 6), position), (shards_of,), jnp.float32, low / len(cuts), high / len(cuts))
        factor_of = factor_of * jnp.repeat(jnp.exp(steps), extent[position] // shards_of).reshape((-1,) + (1,) * (len(extent) - 1 - position))
    return factor_of


def bell_draw(stream_key, extent, scale, bound, cuts=(), kind=jnp.bfloat16):
    drawn = scale * jax.random.normal(stream_key, extent, jnp.float32)
    if cuts:
        drawn = drawn * steps_of(stream_key, extent, cuts, -0.22, 0.18)
    return jnp.clip(drawn, -bound, bound).astype(kind)


def setup_inputs(seed: int = 0) -> dict:
    splits = jax.random.split(jax.random.key(seed), 4)
    seq_embed = draw_seq_embed(jax.random.fold_in(splits[3], 71), 0)
    w_qkv = draw_w_qkv(jax.random.fold_in(splits[3], 71), 0)
    upstream = bell_draw(splits[2], (BATCH, LENGTH, HEADS * HD), 1.0, 6.0, ((0, 16), (1, 16)))
    return {"seq_embed": seq_embed, "w_qkv": w_qkv, "upstream": upstream}


def one_sequence(tokens, w_qkv, grad_out):
    width = HEADS * HD
    score_scale = 1.0 / math.sqrt(HD)
    projected = jnp.dot(tokens, w_qkv, preferred_element_type=jnp.float32).astype(jnp.bfloat16)
    query_heads = projected[:, :width].reshape(LENGTH, HEADS, HD).astype(jnp.float32)
    key_heads = projected[:, width:2 * width].reshape(LENGTH, HEADS, HD).astype(jnp.float32)
    value_heads = projected[:, 2 * width:].reshape(LENGTH, HEADS, HD).astype(jnp.float32)
    scores = jnp.einsum('qhd,khd->hqk', query_heads, key_heads) * score_scale
    peak = lax.optimization_barrier(jnp.max(scores, axis=-1, keepdims=True))
    log_total = peak[..., 0] + jnp.log(lax.optimization_barrier(jnp.sum(jnp.exp(scores - peak), axis=-1)))
    probs = jnp.exp(scores - log_total[..., None])
    probs_low = probs.astype(jnp.bfloat16)
    attended = jnp.einsum('hqk,khd->qhd', probs_low.astype(jnp.float32), value_heads).astype(jnp.bfloat16)
    grad_heads = grad_out.reshape(LENGTH, HEADS, HD).astype(jnp.float32)
    delta_rows = lax.optimization_barrier(jnp.sum(grad_heads * attended.astype(jnp.float32), axis=-1))
    grad_probs = jnp.einsum('qhd,khd->hqk', grad_heads, value_heads)
    grad_scores = (probs * (grad_probs - delta_rows.T[..., None]) * score_scale).astype(jnp.bfloat16)
    grad_scores_wide = grad_scores.astype(jnp.float32)
    grad_queries = jnp.einsum('hqk,khd->qhd', grad_scores_wide, key_heads).astype(jnp.bfloat16)
    grad_keys = jnp.einsum('hqk,qhd->khd', grad_scores_wide, query_heads).astype(jnp.bfloat16)
    grad_values = jnp.einsum('hqk,qhd->khd', probs_low.astype(jnp.float32), grad_heads).astype(jnp.bfloat16)
    grad_proj = jnp.concatenate([grad_queries.reshape(LENGTH, width), grad_keys.reshape(LENGTH, width), grad_values.reshape(LENGTH, width)], axis=1)
    grad_input = lax.dot_general(grad_proj, w_qkv, (((1,), (1,)), ((), ())), preferred_element_type=jnp.float32).astype(jnp.bfloat16)
    return (attended.reshape(LENGTH, width), grad_input, grad_proj)

def add_block(total, pair):
    token_block, grad_block = pair
    part = lax.dot_general(token_block, grad_block, (((0,), (0,)), ((), ())), preferred_element_type=jnp.float32)
    part = lax.optimization_barrier(part.astype(jnp.bfloat16)).astype(jnp.float32)
    return (total + part, None)

def reference(seq_embed, w_qkv, upstream):
    width = HEADS * HD

    def per_sequence(pair):
        return one_sequence(pair[0], w_qkv, pair[1])
    attended, grad_input, grad_proj = lax.map(per_sequence, (seq_embed, upstream))
    token_blocks = seq_embed.reshape(BATCH * N_SEQ, POS_DEV, D)
    grad_blocks = grad_proj.reshape(BATCH * N_SEQ, POS_DEV, 3 * width)
    total, unused = lax.scan(add_block, jnp.zeros((D, 3 * width), jnp.float32), (token_blocks, grad_blocks))
    return (attended, grad_input, total.astype(jnp.bfloat16))
```

```python
import math

import jax
import jax.numpy as jnp
from jax import lax
from jax.experimental import pallas as pl
from jax.experimental.pallas import tpu as pltpu
from jax.sharding import PartitionSpec as P

MESH = pl.DeviceIdType.MESH
BF = jnp.bfloat16
F32 = jnp.float32
ROWS = 192
D = 1536
HEAD = 128
GROUP = 3
GW = GROUP * HEAD
WROWS = 96
HALF_SCALE = 1.0 / math.sqrt(HEAD)
LOG2E = 1.4426950408889634


class Place:
    def __init__(self):
        dp, seq = lax.axis_index("dp"), lax.axis_index("seq")
        self.z, self.yl = lax.rem(dp, 8), lax.div(dp, 8)
        self.c, self.yh, self.x = lax.rem(seq, 2), lax.rem(lax.div(seq, 2), 2), lax.div(seq, 4)

    def device(self, x=None, yh=None, c=None, yl=None, z=None):
        x = self.x if x is None else x
        yh = self.yh if yh is None else yh
        c = self.c if c is None else c
        yl = self.yl if yl is None else yl
        z = self.z if z is None else z
        return (yl * 8 + z, x * 4 + yh * 2 + c)

    def xs(self, dx):
        return lax.rem(self.x + (dx + 4), 4)


class Net:
    def __init__(self, send, recv, local):
        self.send, self.recv, self.local = send, recv, local
        self.n = 0
        self.m = 0
        self.all = []

    def go(self, src, dst, device):
        cp = pltpu.make_async_remote_copy(
            src_ref=src, dst_ref=dst, send_sem=self.send.at[self.n], recv_sem=self.recv.at[self.n],
            device_id=device, device_id_type=MESH,
        )
        self.n += 1
        cp.start()
        self.all.append(cp)
        return cp

    def here(self, src, dst):
        cp = pltpu.make_async_copy(src, dst, self.local.at[self.m])
        self.m += 1
        cp.start()
        return cp

    def drain(self):
        for cp in self.all:
            cp.wait_send()


def greet(devices):
    barrier = pltpu.get_barrier_semaphore()
    for device in devices:
        pl.semaphore_signal(barrier, inc=1, device_id=device, device_id_type=MESH)
    pl.semaphore_wait(barrier, len(devices))


def rows_of(start, size, unit):
    return pl.ds(pl.multiple_of(start, unit), size)


def gather_kernel(x_ref, w_ref, g_ref, x2, w2, g2, qkv, send, recv, local):
    p = Place()
    net = Net(send, recv, local)
    ypair = p.device(yh=1 - p.yh)
    mirror = p.device(yh=1 - p.yh, yl=1 - p.yl)
    right, left, sib = p.device(x=p.xs(1)), p.device(x=p.xs(-1)), p.device(c=1 - p.c)
    greet([ypair, mirror, right, left, sib])

    def wrows(x, yh):
        return w2.at[rows_of((x * 4 + yh * 2 + p.c) * WROWS, WROWS, 32)]

    def wcols(yh, j):
        return w_ref.at[:, rows_of(yh * GW + 2 * GW * j, GW, 128)]

    mine = wrows(p.x, p.yh)
    theirs = [net.go(wcols(1 - p.yh, j), mine.at[:, pl.ds(j * GW, GW)], mirror) for j in range(3)]
    own = [net.here(wcols(p.yh, j), mine.at[:, pl.ds(j * GW, GW)]) for j in range(3)]
    my_rows = rows_of(p.yh * ROWS, ROWS, 64)
    xo = net.go(x_ref, x2.at[my_rows], ypair)
    xl = net.here(x_ref, x2.at[my_rows])
    go = net.go(g_ref.at[:, rows_of((1 - p.yh) * GW, GW, 128)], g2.at[my_rows], ypair)
    gl = net.here(g_ref.at[:, rows_of(p.yh * GW, GW, 128)], g2.at[my_rows])
    for cp in own:
        cp.wait()
    a_right, a_left = net.go(mine, mine, right), net.go(mine, mine, left)
    relays = [net.go(mine, mine, sib)]

    def relay(x, yh):
        block = wrows(x, yh)
        relays.append(net.go(block, block, sib))

    for cp in theirs:
        cp.wait_recv()
    block = wrows(p.x, 1 - p.yh)
    b_right, b_left = net.go(block, block, right), net.go(block, block, left)
    relay(p.x, 1 - p.yh)
    a_right.wait_recv()
    block = wrows(p.xs(-1), p.yh)
    f_right = net.go(block, block, right)
    relay(p.xs(-1), p.yh)
    a_left.wait_recv()
    relay(p.xs(1), p.yh)
    b_left.wait_recv()
    block = wrows(p.xs(1), 1 - p.yh)
    f_left = net.go(block, block, left)
    relay(p.xs(1), 1 - p.yh)
    b_right.wait_recv()
    relay(p.xs(-1), 1 - p.yh)
    f_right.wait_recv()
    relay(p.xs(2), p.yh)
    f_left.wait_recv()
    relay(p.xs(2), 1 - p.yh)
    for cp in (xl, gl):
        cp.wait()
    for cp in (xo, go):
        cp.wait_recv()
    for cp in relays:
        cp.wait_recv()
    for j in range(3):
        cols = pl.ds(j * GW, GW)
        qkv[:, cols] = jnp.dot(x2[...], w2[:, cols], preferred_element_type=F32).astype(BF)
    net.drain()


NT = (((1,), (1,)), ((), ()))


def attention_kernel(qkv, g2, att, dproj, kv, part, other, sibl, land_a, land_b, land_l, land_r,
                     m_ref, l_ref, o_ref, lse_ref, delta_ref, dq_ref, o2, send, recv, local):
    p = Place()
    net = Net(send, recv, local)
    ypair = p.device(yh=1 - p.yh)
    right, left, sib = p.device(x=p.xs(1)), p.device(x=p.xs(-1)), p.device(c=1 - p.c)
    greet([ypair, right, left, sib])
    n = 2 * ROWS

    def block(x, half):
        return kv.at[rows_of(x * 2 * n + p.c * n + half * ROWS, ROWS, 64)]

    def relay(x, half):
        return net.go(block(x, half), block(x, half), sib)

    cps = [net.here(qkv.at[pl.ds(h * ROWS, ROWS), pl.ds(GW, 2 * GW)], block(p.x, h)) for h in range(2)]
    for cp in cps:
        cp.wait()
    a, b = block(p.x, 0), block(p.x, 1)
    a_right, b_left = net.go(a, a, right), net.go(b, b, left)
    b_right, a_left = net.go(b, b, right), net.go(a, a, left)
    relays = [relay(p.x, 0), relay(p.x, 1)]

    m_ref[...] = jnp.full_like(m_ref, -1e30)
    l_ref[...] = jnp.zeros_like(l_ref)
    o_ref[...] = jnp.zeros_like(o_ref)
    c2 = HALF_SCALE * LOG2E

    def load(x, h, which):
        return kv[rows_of(x * 2 * n, 2 * n, 128), pl.ds(which * GW + h * HEAD, HEAD)]

    def forward(x):
        for h in range(GROUP):
            q = qkv[:, pl.ds(h * HEAD, HEAD)]
            s = lax.dot_general(load(x, h, 0), q, NT, preferred_element_type=F32) * c2
            m_old = m_ref[pl.ds(h, 1), :]
            m_new = jnp.maximum(m_old, jnp.max(s, axis=0, keepdims=True))
            alpha = jnp.exp2(m_old - m_new)
            e = jnp.exp2(s - m_new)
            m_ref[pl.ds(h, 1), :] = m_new
            l_ref[pl.ds(h, 1), :] = l_ref[pl.ds(h, 1), :] * alpha + jnp.sum(e, axis=0, keepdims=True)
            hr = pl.ds(h * HEAD, HEAD)
            o_ref[hr, :] = o_ref[hr, :] * alpha + jnp.dot(
                load(x, h, 1).T, e.astype(BF), preferred_element_type=F32)

    for cp in relays:
        cp.wait_recv()
    forward(p.x)
    a_right.wait_recv()
    f_right = net.go(block(p.xs(-1), 0), block(p.xs(-1), 0), right)
    r0 = relay(p.xs(-1), 0)
    b_left.wait_recv()
    f_left = net.go(block(p.xs(1), 1), block(p.xs(1), 1), left)
    r1 = relay(p.xs(1), 1)
    b_right.wait_recv()
    r2 = relay(p.xs(-1), 1)
    a_left.wait_recv()
    r3 = relay(p.xs(1), 0)
    for cp in (r0, r2, r1, r3):
        cp.wait_recv()
    forward(p.xs(-1))
    forward(p.xs(1))
    f_right.wait_recv()
    r4 = relay(p.xs(2), 0)
    f_left.wait_recv()
    r5 = relay(p.xs(2), 1)
    r4.wait_recv()
    r5.wait_recv()
    forward(p.xs(2))

    for h in range(GROUP):
        hr = pl.ds(h * HEAD, HEAD)
        l = l_ref[pl.ds(h, 1), :]
        o = (o_ref[hr, :] / l).astype(BF)
        lse_ref[pl.ds(h, 1), :] = m_ref[pl.ds(h, 1), :] + jnp.log2(l)
        delta_ref[pl.ds(h, 1), :] = jnp.sum(
            o.astype(F32) * g2[:, hr].T.astype(F32), axis=0, keepdims=True)
        o2[:, hr] = o.T
    dq_ref[...] = jnp.zeros_like(dq_ref)
    cols = rows_of(p.yh * GW, GW, 128)
    ao = net.go(o2.at[rows_of((1 - p.yh) * ROWS, ROWS, 64)], att.at[:, cols], ypair)
    al = net.here(o2.at[rows_of(p.yh * ROWS, ROWS, 64)], att.at[:, cols])

    def backward(i, x):
        for h in range(GROUP):
            hr = pl.ds(h * HEAD, HEAD)
            q, g = qkv[:, hr], g2[:, hr]
            k = load(x, h, 0)
            s = lax.dot_general(k, q, NT, preferred_element_type=F32) * c2
            e = jnp.exp2(s - lse_ref[pl.ds(h, 1), :])
            dv = jnp.dot(e.astype(BF), g, preferred_element_type=F32).astype(BF)
            de = lax.dot_general(load(x, h, 1), g, NT, preferred_element_type=F32)
            ds = (e * (de - delta_ref[pl.ds(h, 1), :])).astype(BF)
            dk = (jnp.dot(ds, q, preferred_element_type=F32) * HALF_SCALE).astype(BF)
            dq_ref[hr, :] += jnp.dot(k.T, ds, preferred_element_type=F32)
            vr = pl.ds(GW + h * HEAD, HEAD)
            part[i, 0, :, hr] = dk[:n]
            part[i, 1, :, hr] = dk[n:]
            part[i, 0, :, vr] = dv[:n]
            part[i, 1, :, vr] = dv[n:]
        return net.go(part.at[i, 1 - p.c], sibl.at[i], sib)

    def add(i, rows, *lands):
        t = part[i, p.c, rows].astype(F32) + sibl[i, rows].astype(F32)
        for ref in lands:
            t = t + ref[...].astype(F32)
        return t

    top, bottom = pl.ds(0, ROWS), pl.ds(ROWS, ROWS)
    sb = backward(0, p.xs(2))
    sb.wait_recv()
    other[0] = add(0, pl.ds(0, n)).astype(BF)
    ga = net.go(other.at[0, top], land_a, right)
    gb = net.go(other.at[0, bottom], land_b, left)
    s1 = backward(1, p.xs(1))
    s2 = backward(2, p.xs(-1))
    s1.wait_recv()
    ga.wait_recv()
    other[1, top] = add(1, top, land_a).astype(BF)
    other[1, bottom] = add(1, bottom).astype(BF)
    gl = net.go(other.at[1], land_l, right)
    s2.wait_recv()
    gb.wait_recv()
    other[2, top] = add(2, top).astype(BF)
    other[2, bottom] = add(2, bottom, land_b).astype(BF)
    gr = net.go(other.at[2], land_r, left)
    s3 = backward(3, p.x)
    for h in range(GROUP):
        hr = pl.ds(h * HEAD, HEAD)
        dproj[:, hr] = (dq_ref[hr, :] * HALF_SCALE).astype(BF).T
    s3.wait_recv()
    gl.wait_recv()
    gr.wait_recv()
    dproj[:, pl.ds(GW, 2 * GW)] = add(3, pl.ds(0, n), land_l, land_r).astype(BF)
    al.wait()
    ao.wait_recv()
    net.drain()


def grad_kernel(x2, w2, dproj, gi, gw, part, other, sibl, land_a, land_b, land_l, land_r,
                gi_out, gi_in, y_out, y_in, zbuf, z_in, ybuf, fin, send, recv, local):
    p = Place()
    net = Net(send, recv, local)
    ypair = p.device(yh=1 - p.yh)
    right, left, sib = p.device(x=p.xs(1)), p.device(x=p.xs(-1)), p.device(c=1 - p.c)
    near = p.device(yl=1 - p.yl)
    mirror = p.device(yh=1 - p.yh, yl=1 - p.yl)
    zs = [lax.rem(p.z + d, 8) for d in range(8)]
    greet([ypair, right, left, sib, near, mirror] + [p.device(z=zs[d]) for d in range(1, 8)])

    def term(i, x):
        t = lax.dot_general(x2[:, rows_of(x * GW, GW, 128)], dproj[...], (((0,), (0,)), ((), ())),
                            preferred_element_type=F32).astype(BF)
        for c in range(2):
            for yh in range(2):
                lo = (yh * 2 + c) * WROWS
                part[i, c, yh] = t[lo:lo + WROWS]
        return net.go(part.at[i, 1 - p.c], sibl.at[i], sib)

    def add(i, yh, *lands):
        t = part[i, p.c, yh].astype(F32) + sibl[i, yh].astype(F32)
        for ref in lands:
            t = t + ref.astype(F32)
        return t

    sb = term(0, p.xs(2))
    s1 = term(1, p.xs(1))
    s2 = term(2, p.xs(-1))
    sb.wait_recv()
    for yh in range(2):
        other[0, yh] = add(0, yh).astype(BF)
    ga = net.go(other.at[0, 0], land_a, right)
    gb = net.go(other.at[0, 1], land_b, left)
    far = dproj[rows_of((1 - p.yh) * ROWS, ROWS, 64), :]
    gi_out[...] = lax.dot_general(far, w2[...], NT, preferred_element_type=F32).astype(BF)
    gx = net.go(gi_out, gi_in, ypair)
    s1.wait_recv()
    s2.wait_recv()
    other[1, 1] = add(1, 1).astype(BF)
    other[2, 0] = add(2, 0).astype(BF)
    ga.wait_recv()
    other[1, 0] = add(1, 0, land_a[...]).astype(BF)
    gl = net.go(other.at[1], land_l, right)
    gb.wait_recv()
    other[2, 1] = add(2, 1, land_b[...]).astype(BF)
    gr = net.go(other.at[2], land_r, left)
    s3 = term(3, p.x)
    near_rows = dproj[rows_of(p.yh * ROWS, ROWS, 64), :]
    part_gi = lax.dot_general(near_rows, w2[...], NT, preferred_element_type=F32)
    gx.wait_recv()
    gi[...] = (part_gi + gi_in[...].astype(F32)).astype(BF)
    s3.wait_recv()
    gl.wait_recv()
    gr.wait_recv()
    for yh in range(2):
        y_out[yh] = add(3, yh, land_l[yh], land_r[yh]).astype(BF)
    keep = lax.rem(p.yh + p.yl, 2)
    gy = net.go(y_out.at[1 - keep], y_in, near)
    gy.wait_recv()
    t = (y_out[keep].astype(F32) + y_in[...].astype(F32)).astype(BF)
    for j in range(9):
        zbuf[pl.ds(j * WROWS, WROWS), :] = t[:, j * 128:(j + 1) * 128]
    zbuf[pl.ds(864, 32), :] = jnp.zeros((32, 128), BF)
    zc = [net.go(zbuf.at[rows_of(zs[d] * 112, 112, 16)], z_in.at[d - 1], p.device(z=zs[d])) for d in range(1, 8)]
    t = zbuf[rows_of(p.z * 112, 112, 16), :].astype(F32)
    for d in range(1, 8):
        zc[d - 1].wait_recv()
        t = t + z_in[d - 1].astype(F32)
    ybuf[p.yh, p.yl] = t.astype(BF)
    me = ybuf.at[p.yh, p.yl]
    yc = [net.go(me, me, dev) for dev in (near, ypair, mirror)]
    for cp in yc:
        cp.wait_recv()
    zr = rows_of(p.z * 112, 112, 16)
    for g in range(2):
        fin[g, zr, :] = ybuf[g, lax.rem(p.yh + g, 2)]
    blk = fin.at[:, zr]
    fc = [net.go(blk, blk, p.device(z=zs[d])) for d in range(1, 8)]
    for cp in fc:
        cp.wait_recv()
    for g in range(2):
        for j in range(9):
            col = (j // 3) * 2 * GW + g * GW + (j % 3) * 128
            gw[:, pl.ds(col, 128)] = fin[g, pl.ds(j * WROWS, WROWS), :]
    net.drain()


VMEM = pl.BlockSpec(memory_space=pltpu.VMEM)


def call(kernel, cid, args, outs, scratch, copies, local):
    return pl.pallas_call(
        kernel,
        out_shape=[jax.ShapeDtypeStruct(s, BF) for s in outs],
        in_specs=[VMEM] * len(args),
        out_specs=[VMEM] * len(outs),
        scratch_shapes=[pltpu.VMEM(s, t) for s, t in scratch] + [
            pltpu.SemaphoreType.DMA((copies,)), pltpu.SemaphoreType.DMA((copies,)),
            pltpu.SemaphoreType.DMA((local,))],
        compiler_params=pltpu.CompilerParams(
            collective_id=cid, has_side_effects=True, vmem_limit_bytes=56 * 2**20),
    )(*args)


def on_device(seq_embed, w_qkv, upstream):
    n = 2 * ROWS
    x2, w2, g2, qkv = call(
        gather_kernel, 0, (seq_embed[0], w_qkv, upstream[0]),
        [(n, D), (D, 3 * GW), (n, GW), (n, 3 * GW)], [], 24, 8)
    kvw = 2 * GW
    att, dproj = call(
        attention_kernel, 1, (qkv, g2), [(ROWS, 2 * GW), (n, 3 * GW)],
        [((8 * n, kvw), BF), ((4, 2, n, kvw), BF), ((3, n, kvw), BF), ((4, n, kvw), BF),
         ((ROWS, kvw), BF), ((ROWS, kvw), BF), ((n, kvw), BF), ((n, kvw), BF),
         ((8, n), F32), ((8, n), F32), ((GW, n), F32), ((8, n), F32), ((8, n), F32), ((GW, n), F32),
         ((n, GW), BF)], 24, 4)
    gcol = 3 * GW
    gi, gw = call(
        grad_kernel, 2, (x2, w2, dproj), [(ROWS, D), (WROWS, 6 * GW)],
        [((4, 2, 2, WROWS, gcol), BF), ((3, 2, WROWS, gcol), BF), ((4, 2, WROWS, gcol), BF),
         ((WROWS, gcol), BF), ((WROWS, gcol), BF), ((2, WROWS, gcol), BF), ((2, WROWS, gcol), BF),
         ((ROWS, D), BF), ((ROWS, D), BF), ((2, WROWS, gcol), BF), ((WROWS, gcol), BF),
         ((896, 128), BF), ((7, 112, 128), BF), ((2, 2, 112, 128), BF), ((2, 896, 128), BF)], 32, 4)
    return att[None], gi[None], gw


def solution(mesh):
    placed = (P("dp", "seq", None), P("seq", None), P("dp", "seq", None))
    return jax.shard_map(
        on_device,
        mesh=mesh,
        in_specs=placed,
        out_specs=(P("dp", "seq", None), P("dp", "seq", None), P("seq", None)),
        check_vma=False,
    )
```

```python
import math

import jax
import jax.numpy as jnp
from jax import lax
from jax.experimental import pallas as pl
from jax.experimental.pallas import tpu as pltpu
from jax.sharding import PartitionSpec as P

MESH = pl.DeviceIdType.MESH
BF = jnp.bfloat16
F32 = jnp.float32
ROWS = 192
D = 1536
HEAD = 128
GROUP = 3
GW = GROUP * HEAD
WROWS = 96
HALF_SCALE = 1.0 / math.sqrt(HEAD)
LOG2E = 1.4426950408889634


class Place:
    def __init__(self):
        dp, seq = lax.axis_index("dp"), lax.axis_index("seq")
        self.z, self.yl = lax.rem(dp, 8), lax.div(dp, 8)
        self.c, self.yh, self.x = lax.rem(seq, 2), lax.rem(lax.div(seq, 2), 2), lax.div(seq, 4)

    def device(self, x=None, yh=None, c=None, yl=None, z=None):
        x = self.x if x is None else x
        yh = self.yh if yh is None else yh
        c = self.c if c is None else c
        yl = self.yl if yl is None else yl
        z = self.z if z is None else z
        return (yl * 8 + z, x * 4 + yh * 2 + c)

    def xs(self, dx):
        return lax.rem(self.x + (dx + 4), 4)


class Net:
    def __init__(self, send, recv, local):
        self.send, self.recv, self.local = send, recv, local
        self.n = 0
        self.m = 0
        self.all = []

    def go(self, src, dst, device):
        cp = pltpu.make_async_remote_copy(
            src_ref=src, dst_ref=dst, send_sem=self.send.at[self.n], recv_sem=self.recv.at[self.n],
            device_id=device, device_id_type=MESH,
        )
        self.n += 1
        cp.start()
        self.all.append(cp)
        return cp

    def here(self, src, dst):
        cp = pltpu.make_async_copy(src, dst, self.local.at[self.m])
        self.m += 1
        cp.start()
        return cp

    def drain(self):
        for cp in self.all:
            cp.wait_send()


def greet(devices):
    barrier = pltpu.get_barrier_semaphore()
    for device in devices:
        pl.semaphore_signal(barrier, inc=1, device_id=device, device_id_type=MESH)
    pl.semaphore_wait(barrier, len(devices))


def rows_of(start, size, unit):
    return pl.ds(pl.multiple_of(start, unit), size)


NT = (((1,), (1,)), ((), ()))
TN = (((0,), (0,)), ((), ()))
N = 2 * ROWS
GC = 3 * GW
KW = 2 * GW


def step_kernel(x_ref, w_ref, g_ref, att, gi, gw,
                x2, w2, qg, kv, m_ref, l_ref, o_ref, stat_out, stat_in, lse_ref, delta_ref,
                o_out, o_in, o2, dq_ref, dq_out, dq_in, kpart, kother, ksib, kland, dproj,
                part, other, sibl, land_a, land_b, land_l, land_r,
                gi_out, gi_in, y_out, y_in, zbuf, z_in, ybuf, fin, send, recv, local):
    p = Place()
    net = Net(send, recv, local)
    ypair = p.device(yh=1 - p.yh)
    mirror = p.device(yh=1 - p.yh, yl=1 - p.yl)
    near = p.device(yl=1 - p.yl)
    right, left, sib = p.device(x=p.xs(1)), p.device(x=p.xs(-1)), p.device(c=1 - p.c)
    odd = lax.rem(p.x, 2)
    qpair, kpair = p.device(x=p.xs(1 - 2 * odd)), p.device(x=p.xs(2 * odd - 1))
    zs = [lax.rem(p.z + d, 8) for d in range(8)]
    greet([ypair, mirror, near, right, left, sib] + [p.device(z=zs[d]) for d in range(1, 8)])

    def wrows(x, yh):
        return w2.at[rows_of((x * 4 + yh * 2 + p.c) * WROWS, WROWS, 32)]

    def wcols(yh, j):
        return w_ref.at[:, rows_of(yh * GW + 2 * GW * j, GW, 128)]

    mine = wrows(p.x, p.yh)
    theirs = [net.go(wcols(1 - p.yh, j), mine.at[:, pl.ds(j * GW, GW)], mirror) for j in range(3)]
    own = [net.here(wcols(p.yh, j), mine.at[:, pl.ds(j * GW, GW)]) for j in range(3)]
    my_rows = rows_of(p.yh * ROWS, ROWS, 64)
    far_rows = rows_of((1 - p.yh) * ROWS, ROWS, 64)
    for cp in own:
        cp.wait()
    a_right, a_left = net.go(mine, mine, right), net.go(mine, mine, left)
    relays = [net.go(mine, mine, sib)]

    def relay(x, yh):
        block = wrows(x, yh)
        relays.append(net.go(block, block, sib))

    qg[my_rows, pl.ds(GW, GW)] = g_ref[:, rows_of(p.yh * GW, GW, 128)]
    for cp in theirs:
        cp.wait_recv()
    xo = net.go(x_ref, x2.at[my_rows], ypair)
    block = wrows(p.x, 1 - p.yh)
    b_right, b_left = net.go(block, block, right), net.go(block, block, left)
    relay(p.x, 1 - p.yh)
    a_right.wait_recv()
    block = wrows(p.xs(-1), p.yh)
    f_right = net.go(block, block, right)
    relay(p.xs(-1), p.yh)
    a_left.wait_recv()
    relay(p.xs(1), p.yh)
    b_left.wait_recv()
    block = wrows(p.xs(1), 1 - p.yh)
    f_left = net.go(block, block, left)
    relay(p.xs(1), 1 - p.yh)
    b_right.wait_recv()
    relay(p.xs(-1), 1 - p.yh)
    go = net.go(g_ref.at[:, rows_of((1 - p.yh) * GW, GW, 128)], qg.at[my_rows, pl.ds(GW, GW)], ypair)
    f_right.wait_recv()
    relay(p.xs(2), p.yh)
    f_left.wait_recv()
    relay(p.xs(2), 1 - p.yh)
    for cp in relays:
        cp.wait_recv()

    def project(tokens, rows, j):
        t = jnp.dot(tokens[...], w2[:, pl.ds(j * GW, GW)], preferred_element_type=F32).astype(BF)
        if j == 0:
            qg[rows, pl.ds(0, GW)] = t
        else:
            kv[0, p.c, rows, pl.ds((j - 1) * GW, GW)] = t

    def give(rows):
        mk, mq = kv.at[0, p.c, rows], qg.at[rows]
        out = [net.go(mk, kv.at[1, p.c, rows], kpair), net.go(mk, mk, sib)]
        return out, mq

    project(x_ref, my_rows, 1)
    project(x_ref, my_rows, 2)
    (k_a, s_a), mq = give(my_rows)
    project(x_ref, my_rows, 0)
    there = rows_of(N + p.yh * ROWS, ROWS, 64)
    q_a = net.go(mq, qg.at[there], qpair)
    xo.wait_recv()
    far_x = x2.at[far_rows]
    project(far_x, far_rows, 1)
    project(far_x, far_rows, 2)
    (k_b, s_b), mq = give(far_rows)
    project(far_x, far_rows, 0)
    go.wait_recv()
    q_b = net.go(mq, qg.at[rows_of(N + (1 - p.yh) * ROWS, ROWS, 64)], qpair)
    x2[my_rows, :] = x_ref[...]

    m_ref[...] = jnp.full_like(m_ref, -1e30)
    l_ref[...] = jnp.zeros_like(l_ref)
    o_ref[...] = jnp.zeros_like(o_ref)
    c2 = HALF_SCALE * LOG2E

    def load(b, h, which):
        return kv[b, :, :, pl.ds(which * GW + h * HEAD, HEAD)].reshape(2 * N, HEAD)

    def forward(b, lo, size):
        qr = pl.ds(lo, size)
        for h in range(GROUP):
            q = qg[qr, pl.ds(h * HEAD, HEAD)]
            s = lax.dot_general(load(b, h, 0), q, NT, preferred_element_type=F32) * c2
            hs, hr = pl.ds(h, 1), pl.ds(h * HEAD, HEAD)
            m_old = m_ref[hs, qr]
            m_new = jnp.maximum(m_old, jnp.max(s, axis=0, keepdims=True))
            alpha = jnp.exp2(m_old - m_new)
            e = jnp.exp2(s - m_new)
            m_ref[hs, qr] = m_new
            l_ref[hs, qr] = l_ref[hs, qr] * alpha + jnp.sum(e, axis=0, keepdims=True)
            o_ref[hr, qr] = o_ref[hr, qr] * alpha + jnp.dot(
                load(b, h, 1).T, e.astype(BF), preferred_element_type=F32)

    s_a.wait_recv()
    s_b.wait_recv()
    forward(0, 0, N)
    k_a.wait_recv()
    t_a = net.go(kv.at[1, p.c, my_rows], kv.at[1, p.c, my_rows], sib)
    q_a.wait_recv()
    q_b.wait_recv()
    forward(0, N, N)
    k_b.wait_recv()
    t_b = net.go(kv.at[1, p.c, far_rows], kv.at[1, p.c, far_rows], sib)
    t_a.wait_recv()
    t_b.wait_recv()
    forward(1, 0, 2 * N)

    stat_out[...] = jnp.zeros_like(stat_out)
    for h in range(GROUP):
        hr = pl.ds(h * HEAD, HEAD)
        stat_out[pl.ds(h, 1), :] = m_ref[pl.ds(h, 1), :]
        stat_out[pl.ds(GROUP + h, 1), :] = l_ref[pl.ds(h, 1), :]
        stat_out[pl.ds(2 * GROUP + h, 1), :] = jnp.sum(
            o_ref[hr, :] * qg[:, pl.ds(GW + h * HEAD, HEAD)].T.astype(F32), axis=0, keepdims=True)
    st = net.go(stat_out, stat_in, qpair)
    st.wait_recv()

    def stat(i):
        other_half = stat_in[pl.ds(i, 1), :]
        return stat_out[pl.ds(i, 1), :], jnp.concatenate([other_half[:, N:], other_half[:, :N]], axis=1)

    for h in range(GROUP):
        hs = pl.ds(h, 1)
        m1, m2 = stat(h)
        l1, l2 = stat(GROUP + h)
        d1, d2 = stat(2 * GROUP + h)
        m = jnp.maximum(m1, m2)
        f1, f2 = jnp.exp2(m1 - m), jnp.exp2(m2 - m)
        l = l1 * f1 + l2 * f2
        lse_ref[hs, :] = m + jnp.log2(l)
        delta_ref[hs, :] = (d1 * f1 + d2 * f2) / l
        l_ref[hs, :] = f1 / l
    dq_ref[...] = jnp.zeros_like(dq_ref)

    def backward(i, b, h):
        hr = pl.ds(h * HEAD, HEAD)
        q, g = qg[:, hr], qg[:, pl.ds(GW + h * HEAD, HEAD)]
        k = load(b, h, 0)
        s = lax.dot_general(k, q, NT, preferred_element_type=F32) * c2
        e = jnp.exp2(s - lse_ref[pl.ds(h, 1), :])
        dv = jnp.dot(e.astype(BF), g, preferred_element_type=F32).astype(BF)
        de = lax.dot_general(load(b, h, 1), g, NT, preferred_element_type=F32)
        ds = (e * (de - delta_ref[pl.ds(h, 1), :])).astype(BF)
        dk = (jnp.dot(ds, q, preferred_element_type=F32) * HALF_SCALE).astype(BF)
        dq_ref[hr, :] += jnp.dot(k.T, ds, preferred_element_type=F32)
        for c in range(2):
            kpart[i, h, c, :, pl.ds(0, HEAD)] = dk[c * N:(c + 1) * N]
            kpart[i, h, c, :, pl.ds(HEAD, HEAD)] = dv[c * N:(c + 1) * N]
        return net.go(kpart.at[i, h, 1 - p.c], ksib.at[i, h], sib)

    def pass_on(h, cp):
        cp.wait_recv()
        kother[h] = (kpart[0, h, p.c].astype(F32) + ksib[0, h].astype(F32)).astype(BF)
        return net.go(kother.at[h], kland.at[h], kpair)

    k0 = backward(0, 1, 0)
    k1 = backward(0, 1, 1)
    lands = [pass_on(0, k0)]
    k2 = backward(0, 1, 2)
    lands.append(pass_on(1, k1))
    for h in range(GROUP):
        hr = pl.ds(h * HEAD, HEAD)
        o_ref[hr, :] = o_ref[hr, :] * l_ref[pl.ds(h, 1), :]
        o_out[hr, :] = o_ref[hr, pl.ds(N, N)].astype(BF)
    oc = net.go(o_out, o_in, qpair)
    lands.append(pass_on(2, k2))
    own_k, dqs = [], []
    for h in range(GROUP):
        hr = pl.ds(h * HEAD, HEAD)
        own_k.append(backward(1, 0, h))
        dq_out[hr, :] = (dq_ref[hr, pl.ds(N, N)] * HALF_SCALE).astype(BF)
        dqs.append(net.go(dq_out.at[hr], dq_in.at[hr], qpair))
    oc.wait_recv()
    for h in range(GROUP):
        hr = pl.ds(h * HEAD, HEAD)
        o2[:, hr] = (o_ref[hr, pl.ds(0, N)] + o_in[hr, :].astype(F32)).astype(BF).T
    cols = rows_of(p.yh * GW, GW, 128)
    ao = net.go(o2.at[far_rows], att.at[:, cols], ypair)
    al = net.here(o2.at[my_rows], att.at[:, cols])
    for h in range(GROUP):
        hr = pl.ds(h * HEAD, HEAD)
        dqs[h].wait_recv()
        dproj[:, hr] = (dq_ref[hr, pl.ds(0, N)] * HALF_SCALE + dq_in[hr, :].astype(F32)).astype(BF).T
    for h in range(GROUP):
        own_k[h].wait_recv()
        lands[h].wait_recv()
        t = kpart[1, h, p.c].astype(F32) + ksib[1, h].astype(F32) + kland[h].astype(F32)
        dproj[:, pl.ds(GW + h * HEAD, HEAD)] = t[:, :HEAD].astype(BF)
        dproj[:, pl.ds(2 * GW + h * HEAD, HEAD)] = t[:, HEAD:].astype(BF)

    def term(i, x):
        t = lax.dot_general(x2[:, rows_of(x * GW, GW, 128)], dproj[...], (((0,), (0,)), ((), ())),
                            preferred_element_type=F32).astype(BF)
        for c in range(2):
            for yh in range(2):
                lo = (yh * 2 + c) * WROWS
                part[i, c, yh] = t[lo:lo + WROWS]
        return net.go(part.at[i, 1 - p.c], sibl.at[i], sib)

    def add(i, yh, *lands):
        t = part[i, p.c, yh].astype(F32) + sibl[i, yh].astype(F32)
        for ref in lands:
            t = t + ref.astype(F32)
        return t

    sb = term(0, p.xs(2))
    s1 = term(1, p.xs(1))
    s2 = term(2, p.xs(-1))
    sb.wait_recv()
    for yh in range(2):
        other[0, yh] = add(0, yh).astype(BF)
    ga = net.go(other.at[0, 0], land_a, right)
    gb = net.go(other.at[0, 1], land_b, left)
    far = dproj[far_rows, :]
    gi_out[...] = lax.dot_general(far, w2[...], NT, preferred_element_type=F32).astype(BF)
    gx = net.go(gi_out, gi_in, ypair)
    s1.wait_recv()
    s2.wait_recv()
    other[1, 1] = add(1, 1).astype(BF)
    other[2, 0] = add(2, 0).astype(BF)
    ga.wait_recv()
    other[1, 0] = add(1, 0, land_a[...]).astype(BF)
    gl = net.go(other.at[1], land_l, right)
    gb.wait_recv()
    other[2, 1] = add(2, 1, land_b[...]).astype(BF)
    gr = net.go(other.at[2], land_r, left)
    s3 = term(3, p.x)
    near_rows = dproj[my_rows, :]
    part_gi = lax.dot_general(near_rows, w2[...], NT, preferred_element_type=F32)
    gx.wait_recv()
    gi[...] = (part_gi + gi_in[...].astype(F32)).astype(BF)
    s3.wait_recv()
    gl.wait_recv()
    gr.wait_recv()
    for yh in range(2):
        y_out[yh] = add(3, yh, land_l[yh], land_r[yh]).astype(BF)
    keep = lax.rem(p.yh + p.yl, 2)
    gy = net.go(y_out.at[1 - keep], y_in, near)
    gy.wait_recv()
    t = (y_out[keep].astype(F32) + y_in[...].astype(F32)).astype(BF)
    for j in range(9):
        zbuf[pl.ds(j * WROWS, WROWS), :] = t[:, j * 128:(j + 1) * 128]
    zbuf[pl.ds(864, 32), :] = jnp.zeros((32, 128), BF)
    zc = [net.go(zbuf.at[rows_of(zs[d] * 112, 112, 16)], z_in.at[d - 1], p.device(z=zs[d])) for d in range(1, 8)]
    t = zbuf[rows_of(p.z * 112, 112, 16), :].astype(F32)
    for d in range(1, 8):
        zc[d - 1].wait_recv()
        t = t + z_in[d - 1].astype(F32)
    ybuf[p.yh, p.yl] = t.astype(BF)
    me = ybuf.at[p.yh, p.yl]
    yc = [net.go(me, me, dev) for dev in (near, ypair, mirror)]
    for cp in yc:
        cp.wait_recv()
    zr = rows_of(p.z * 112, 112, 16)
    for g in range(2):
        fin[g, zr, :] = ybuf[g, lax.rem(p.yh + g, 2)]
    blk = fin.at[:, zr]
    fc = [net.go(blk, blk, p.device(z=zs[d])) for d in range(1, 8)]
    for cp in fc:
        cp.wait_recv()
    for g in range(2):
        for j in range(9):
            col = (j // 3) * 2 * GW + g * GW + (j % 3) * 128
            gw[:, pl.ds(col, 128)] = fin[g, pl.ds(j * WROWS, WROWS), :]
    al.wait()
    ao.wait_recv()
    net.drain()


VMEM = pl.BlockSpec(memory_space=pltpu.VMEM)


def on_device(seq_embed, w_qkv, upstream):
    scratch = [
        ((N, D), BF), ((D, GC), BF), ((2 * N, KW), BF), ((2, 2, N, KW), BF),
        ((8, 2 * N), F32), ((8, 2 * N), F32), ((GW, 2 * N), F32), ((16, 2 * N), F32), ((16, 2 * N), F32),
        ((8, 2 * N), F32), ((8, 2 * N), F32),
        ((GW, N), BF), ((GW, N), BF), ((N, GW), BF), ((GW, 2 * N), F32), ((GW, N), BF), ((GW, N), BF),
        ((2, GROUP, 2, N, 2 * HEAD), BF), ((GROUP, N, 2 * HEAD), BF), ((2, GROUP, N, 2 * HEAD), BF),
        ((GROUP, N, 2 * HEAD), BF), ((N, GC), BF),
        ((4, 2, 2, WROWS, GC), BF), ((3, 2, WROWS, GC), BF), ((4, 2, WROWS, GC), BF),
        ((WROWS, GC), BF), ((WROWS, GC), BF), ((2, WROWS, GC), BF), ((2, WROWS, GC), BF),
        ((ROWS, D), BF), ((ROWS, D), BF), ((2, WROWS, GC), BF), ((WROWS, GC), BF),
        ((896, 128), BF), ((7, 112, 128), BF), ((2, 2, 112, 128), BF), ((2, 896, 128), BF),
    ]
    copies = 80
    att, gi, gw = pl.pallas_call(
        step_kernel,
        out_shape=[jax.ShapeDtypeStruct(s, BF) for s in ((ROWS, KW), (ROWS, D), (WROWS, 2 * GC))],
        in_specs=[VMEM] * 3,
        out_specs=[VMEM] * 3,
        scratch_shapes=[pltpu.VMEM(s, t) for s, t in scratch] + [
            pltpu.SemaphoreType.DMA((copies,)), pltpu.SemaphoreType.DMA((copies,)),
            pltpu.SemaphoreType.DMA((8,))],
        compiler_params=pltpu.CompilerParams(
            collective_id=0, has_side_effects=True, vmem_limit_bytes=58 * 2**20),
    )(seq_embed[0], w_qkv, upstream[0])
    return att[None], gi[None], gw


def solution(mesh):
    placed = (P("dp", "seq", None), P("seq", None), P("dp", "seq", None))
    return jax.shard_map(
        on_device,
        mesh=mesh,
        in_specs=placed,
        out_specs=(P("dp", "seq", None), P("dp", "seq", None), P("seq", None)),
        check_vma=False,
    )
```

```python
import math

import jax
import jax.numpy as jnp
from jax import lax
from jax.experimental import pallas as pl
from jax.experimental.pallas import tpu as pltpu
from jax.sharding import PartitionSpec as P

MESH = pl.DeviceIdType.MESH
BF = jnp.bfloat16
F32 = jnp.float32
ROWS = 192
D = 1536
HEAD = 128
GROUP = 3
GW = GROUP * HEAD
WROWS = 96
HALF_SCALE = 1.0 / math.sqrt(HEAD)
LOG2E = 1.4426950408889634


class Place:
    def __init__(self):
        dp, seq = lax.axis_index("dp"), lax.axis_index("seq")
        self.z, self.yl = lax.rem(dp, 8), lax.div(dp, 8)
        self.c, self.yh, self.x = lax.rem(seq, 2), lax.rem(lax.div(seq, 2), 2), lax.div(seq, 4)

    def device(self, x=None, yh=None, c=None, yl=None, z=None):
        x = self.x if x is None else x
        yh = self.yh if yh is None else yh
        c = self.c if c is None else c
        yl = self.yl if yl is None else yl
        z = self.z if z is None else z
        return (yl * 8 + z, x * 4 + yh * 2 + c)

    def xs(self, dx):
        return lax.rem(self.x + (dx + 4), 4)


class Net:
    def __init__(self, send, recv, local):
        self.send, self.recv, self.local = send, recv, local
        self.n = 0
        self.m = 0
        self.all = []

    def go(self, src, dst, device):
        cp = pltpu.make_async_remote_copy(
            src_ref=src, dst_ref=dst, send_sem=self.send.at[self.n], recv_sem=self.recv.at[self.n],
            device_id=device, device_id_type=MESH,
        )
        self.n += 1
        cp.start()
        self.all.append(cp)
        return cp

    def make(self, src, dst, device):
        self.n += 1
        return pltpu.make_async_remote_copy(
            src_ref=src, dst_ref=dst, send_sem=self.send.at[self.n - 1], recv_sem=self.recv.at[self.n - 1],
            device_id=device, device_id_type=MESH,
        )

    def here(self, src, dst):
        cp = pltpu.make_async_copy(src, dst, self.local.at[self.m])
        self.m += 1
        cp.start()
        return cp

    def drain(self):
        for cp in self.all:
            cp.wait_send()


def greet(devices):
    barrier = pltpu.get_barrier_semaphore()
    for device in devices:
        pl.semaphore_signal(barrier, inc=1, device_id=device, device_id_type=MESH)
    pl.semaphore_wait(barrier, len(devices))


def rows_of(start, size, unit):
    return pl.ds(pl.multiple_of(start, unit), size)


NT = (((1,), (1,)), ((), ()))
TN = (((0,), (0,)), ((), ()))
N = 2 * ROWS
GC = 3 * GW
KW = 2 * GW


def step_kernel(x_ref, w_ref, g_ref, att, gi, gw,
                x2, w2, qg, kv, m_ref, l_ref, o_ref, stat_out, stat_in, lse_ref, delta_ref,
                o_out, o_in, o2, dq_ref, dq_out, dq_in, kpart, kother, ksib, kland, dproj,
                part, other, sibl, land_a, land_b, land_l, land_r,
                dfar, w3, zbuf, z_in, own, fin, send, recv, local):
    p = Place()
    net = Net(send, recv, local)
    ypair = p.device(yh=1 - p.yh)
    mirror = p.device(yh=1 - p.yh, yl=1 - p.yl)
    near = p.device(yl=1 - p.yl)
    right, left, sib = p.device(x=p.xs(1)), p.device(x=p.xs(-1)), p.device(c=1 - p.c)
    odd = lax.rem(p.x, 2)
    qpair, kpair = p.device(x=p.xs(1 - 2 * odd)), p.device(x=p.xs(2 * odd - 1))
    zs = [lax.rem(p.z + d, 8) for d in range(8)]
    greet([right, left, sib] + [
        p.device(yh=p.yh if a == 0 else 1 - p.yh, yl=p.yl if b == 0 else 1 - p.yl, z=zs[d])
        for d in range(8) for a in range(2) for b in range(2) if d + a + b > 0])

    def wrows(x, yh):
        return w2.at[rows_of((x * 4 + yh * 2 + p.c) * WROWS, WROWS, 32)]

    def wcols(yh, j):
        return w_ref.at[:, rows_of(yh * GW + 2 * GW * j, GW, 128)]

    mine = wrows(p.x, p.yh)
    theirs = [net.go(wcols(1 - p.yh, j), mine.at[:, pl.ds(j * GW, GW)], mirror) for j in range(3)]
    own_w = [net.here(wcols(p.yh, j), mine.at[:, pl.ds(j * GW, GW)]) for j in range(3)]
    my_rows = rows_of(p.yh * ROWS, ROWS, 64)
    far_rows = rows_of((1 - p.yh) * ROWS, ROWS, 64)
    for cp in own_w:
        cp.wait()
    a_right, a_left = net.go(mine, mine, right), net.go(mine, mine, left)
    relays = [net.go(mine, mine, sib)]

    def relay(x, yh):
        block = wrows(x, yh)
        relays.append(net.go(block, block, sib))

    qg[my_rows, pl.ds(GW, GW)] = g_ref[:, rows_of(p.yh * GW, GW, 128)]
    for cp in theirs:
        cp.wait_recv()
    xo = net.go(x_ref, x2.at[my_rows], ypair)
    block = wrows(p.x, 1 - p.yh)
    b_right, b_left = net.go(block, block, right), net.go(block, block, left)
    relay(p.x, 1 - p.yh)
    a_right.wait_recv()
    block = wrows(p.xs(-1), p.yh)
    f_right = net.go(block, block, right)
    relay(p.xs(-1), p.yh)
    a_left.wait_recv()
    relay(p.xs(1), p.yh)
    b_left.wait_recv()
    block = wrows(p.xs(1), 1 - p.yh)
    f_left = net.go(block, block, left)
    relay(p.xs(1), 1 - p.yh)
    b_right.wait_recv()
    relay(p.xs(-1), 1 - p.yh)
    go = net.go(g_ref.at[:, rows_of((1 - p.yh) * GW, GW, 128)], qg.at[my_rows, pl.ds(GW, GW)], ypair)
    f_right.wait_recv()
    relay(p.xs(2), p.yh)
    f_left.wait_recv()
    relay(p.xs(2), 1 - p.yh)
    for cp in relays:
        cp.wait_recv()

    half_w = rows_of(p.c * (D // 2), D // 2, 256)

    def project(tokens, rows, j):
        t = jnp.dot(tokens[...], w2[:, pl.ds(j * GW, GW)], preferred_element_type=F32).astype(BF)
        if j == 0:
            qg[rows, pl.ds(0, GW)] = t
        else:
            kv[0, p.c, rows, pl.ds((j - 1) * GW, GW)] = t

    def give(rows):
        mk, mq = kv.at[0, p.c, rows], qg.at[rows, pl.ds(0, GW)]
        out = [net.go(mk, kv.at[1, p.c, rows], kpair), net.go(mk, mk, sib)]
        return out, mq

    project(x_ref, my_rows, 1)
    project(x_ref, my_rows, 2)
    (k_a, s_a), mq = give(my_rows)
    project(x_ref, my_rows, 0)
    there = rows_of(N + p.yh * ROWS, ROWS, 64)
    q_a = net.go(mq, qg.at[there, pl.ds(0, GW)], qpair)
    xo.wait_recv()
    far_x = x2.at[far_rows]
    project(far_x, far_rows, 1)
    project(far_x, far_rows, 2)
    (k_b, s_b), mq = give(far_rows)
    project(far_x, far_rows, 0)
    there_b = rows_of(N + (1 - p.yh) * ROWS, ROWS, 64)
    q_b = net.go(mq, qg.at[there_b, pl.ds(0, GW)], qpair)
    g_cols = pl.ds(GW, GW)
    g_a = net.go(qg.at[my_rows, g_cols], qg.at[there, g_cols], qpair)
    go.wait_recv()
    g_b = net.go(qg.at[far_rows, g_cols], qg.at[there_b, g_cols], qpair)
    w_far = net.go(w2.at[half_w], w3.at[half_w], mirror)
    x2[my_rows, :] = x_ref[...]

    m_ref[...] = jnp.full_like(m_ref, -1e30)
    l_ref[...] = jnp.zeros_like(l_ref)
    o_ref[...] = jnp.zeros_like(o_ref)
    c2 = HALF_SCALE * LOG2E

    def forward(b, rows, lo, size):
        qr = pl.ds(lo, size)
        for h in range(GROUP):
            q = qg[qr, pl.ds(h * HEAD, HEAD)]
            keys = kv[b, :, rows, pl.ds(h * HEAD, HEAD)].reshape(N, HEAD)
            values = kv[b, :, rows, pl.ds(GW + h * HEAD, HEAD)].reshape(N, HEAD)
            s = lax.dot_general(keys, q, NT, preferred_element_type=F32) * c2
            hs, hr = pl.ds(h, 1), pl.ds(h * HEAD, HEAD)
            m_old = m_ref[hs, qr]
            m_new = jnp.maximum(m_old, jnp.max(s, axis=0, keepdims=True))
            alpha = jnp.exp2(m_old - m_new)
            e = jnp.exp2(s - m_new)
            m_ref[hs, qr] = m_new
            l_ref[hs, qr] = l_ref[hs, qr] * alpha + jnp.sum(e, axis=0, keepdims=True)
            o_ref[hr, qr] = o_ref[hr, qr] * alpha + jnp.dot(
                values.T, e.astype(BF), preferred_element_type=F32)

    s_a.wait_recv()
    forward(0, my_rows, 0, N)
    s_b.wait_recv()
    forward(0, far_rows, 0, N)
    k_a.wait_recv()
    t_a = net.go(kv.at[1, p.c, my_rows], kv.at[1, p.c, my_rows], sib)
    t_a.wait_recv()
    forward(1, my_rows, 0, N)
    q_a.wait_recv()
    q_b.wait_recv()
    forward(0, my_rows, N, N)
    forward(0, far_rows, N, N)
    forward(1, my_rows, N, N)
    k_b.wait_recv()
    t_b = net.go(kv.at[1, p.c, far_rows], kv.at[1, p.c, far_rows], sib)
    g_a.wait_recv()
    g_b.wait_recv()
    t_b.wait_recv()
    forward(1, far_rows, 0, 2 * N)

    stat_out[...] = jnp.zeros_like(stat_out)
    for h in range(GROUP):
        hr = pl.ds(h * HEAD, HEAD)
        stat_out[pl.ds(h, 1), :] = m_ref[pl.ds(h, 1), :]
        stat_out[pl.ds(GROUP + h, 1), :] = l_ref[pl.ds(h, 1), :]
        stat_out[pl.ds(2 * GROUP + h, 1), :] = jnp.sum(
            o_ref[hr, :] * qg[:, pl.ds(GW + h * HEAD, HEAD)].T.astype(F32), axis=0, keepdims=True)
    st = net.go(stat_out, stat_in, qpair)
    st.wait_recv()

    def stat(i):
        other_half = stat_in[pl.ds(i, 1), :]
        return stat_out[pl.ds(i, 1), :], jnp.concatenate([other_half[:, N:], other_half[:, :N]], axis=1)

    for h in range(GROUP):
        hs = pl.ds(h, 1)
        m1, m2 = stat(h)
        l1, l2 = stat(GROUP + h)
        d1, d2 = stat(2 * GROUP + h)
        m = jnp.maximum(m1, m2)
        f1, f2 = jnp.exp2(m1 - m), jnp.exp2(m2 - m)
        l = l1 * f1 + l2 * f2
        lse_ref[hs, :] = m + jnp.log2(l)
        delta_ref[hs, :] = (d1 * f1 + d2 * f2) / l
        l_ref[hs, :] = f1 / l
    dq_ref[...] = jnp.zeros_like(dq_ref)

    def backward(i, b, h, own_core):
        hr = pl.ds(h * HEAD, HEAD)
        c = p.c if own_core else 1 - p.c
        q, g = qg[:, hr], qg[:, pl.ds(GW + h * HEAD, HEAD)]
        k = kv[b, c, :, hr]
        s = lax.dot_general(k, q, NT, preferred_element_type=F32) * c2
        e = jnp.exp2(s - lse_ref[pl.ds(h, 1), :])
        dv = jnp.dot(e.astype(BF), g, preferred_element_type=F32).astype(BF)
        de = lax.dot_general(kv[b, c, :, pl.ds(GW + h * HEAD, HEAD)], g, NT, preferred_element_type=F32)
        ds = (e * (de - delta_ref[pl.ds(h, 1), :])).astype(BF)
        dk = (jnp.dot(ds, q, preferred_element_type=F32) * HALF_SCALE).astype(BF)
        dq_ref[hr, :] += jnp.dot(k.T, ds, preferred_element_type=F32)
        kpart[i, h, own_core, :, pl.ds(0, HEAD)] = dk
        kpart[i, h, own_core, :, pl.ds(HEAD, HEAD)] = dv
        return None if own_core else net.go(kpart.at[i, h, 0], ksib.at[i, h], sib)

    for h in range(GROUP):
        hr = pl.ds(h * HEAD, HEAD)
        o_ref[hr, :] = o_ref[hr, :] * l_ref[pl.ds(h, 1), :]
        o_out[hr, :] = o_ref[hr, pl.ds(N, N)].astype(BF)
    oc = net.go(o_out, o_in, qpair)
    lands = []
    for h in range(GROUP):
        cp = backward(0, 1, h, 0)
        backward(0, 1, h, 1)
        cp.wait_recv()
        kother[h] = (kpart[0, h, 1].astype(F32) + ksib[0, h].astype(F32)).astype(BF)
        lands.append(net.go(kother.at[h], kland.at[h], kpair))
    own_k, dqs = [], []
    for h in range(GROUP):
        hr = pl.ds(h * HEAD, HEAD)
        own_k.append(backward(1, 0, h, 0))
        backward(1, 0, h, 1)
        dq_out[hr, :] = (dq_ref[hr, pl.ds(N, N)] * HALF_SCALE).astype(BF)
        dqs.append(net.go(dq_out.at[hr], dq_in.at[hr], qpair))
    oc.wait_recv()
    for h in range(GROUP):
        hr = pl.ds(h * HEAD, HEAD)
        o2[:, hr] = (o_ref[hr, pl.ds(0, N)] + o_in[hr, :].astype(F32)).astype(BF).T
    cols = rows_of(p.yh * GW, GW, 128)
    ao = net.go(o2.at[far_rows], att.at[:, cols], ypair)
    al = net.here(o2.at[my_rows], att.at[:, cols])
    for h in range(GROUP):
        hr = pl.ds(h * HEAD, HEAD)
        dqs[h].wait_recv()
        dproj[:, hr] = (dq_ref[hr, pl.ds(0, N)] * HALF_SCALE + dq_in[hr, :].astype(F32)).astype(BF).T

    order = [p.xs(2), p.xs(1), p.xs(-1), p.x]
    jobs = [{} for _ in range(3)]

    def terms(j):
        jobs[j]["sib"] = []
        for i, x in enumerate(order):
            t = lax.dot_general(x2[:, rows_of(x * GW, GW, 128)], dproj[:, pl.ds(j * GW, GW)], TN,
                                preferred_element_type=F32).astype(BF)
            for c in range(2):
                for yh in range(2):
                    lo = (yh * 2 + c) * WROWS
                    part[j, i, c, yh] = t[lo:lo + WROWS]
            jobs[j]["sib"].append(net.go(part.at[j, i, 1 - p.c], sibl.at[j, i], sib))

    def add(j, i, yh, *lands):
        t = part[j, i, p.c, yh].astype(F32) + sibl[j, i, yh].astype(F32)
        for ref in lands:
            t = t + ref.astype(F32)
        return t

    def x_first(j):
        jobs[j]["sib"][0].wait_recv()
        for yh in range(2):
            other[j, 0, yh] = add(j, 0, yh).astype(BF)
        jobs[j]["a"] = net.go(other.at[j, 0, 0], land_a.at[j], right)
        jobs[j]["b"] = net.go(other.at[j, 0, 1], land_b.at[j], left)

    def x_second(j):
        job = jobs[j]
        job["sib"][1].wait_recv()
        job["sib"][2].wait_recv()
        other[j, 1, 1] = add(j, 1, 1).astype(BF)
        other[j, 2, 0] = add(j, 2, 0).astype(BF)
        job["a"].wait_recv()
        other[j, 1, 0] = add(j, 1, 0, land_a[j]).astype(BF)
        job["l"] = net.go(other.at[j, 1], land_l.at[j], right)
        job["b"].wait_recv()
        other[j, 2, 1] = add(j, 2, 1, land_b[j]).astype(BF)
        job["r"] = net.go(other.at[j, 2], land_r.at[j], left)

    def peer(yl, d, yh=None):
        return p.device(yh=yh, yl=yl, z=zs[d])

    def piece(z):
        return rows_of(z * 48, 48, 16)

    def dp_sum(j):
        job = jobs[j]
        job["sib"][3].wait_recv()
        job["l"].wait_recv()
        job["r"].wait_recv()
        for r in range(2):
            t = add(j, 3, r, land_l[j, r], land_r[j, r]).astype(BF)
            for i in range(3):
                zbuf[j, r, pl.ds(i * WROWS, WROWS), :] = t[:, i * 128:(i + 1) * 128]
        job["z"] = []
        for d in (4, 3, 5, 2, 6, 1, 7, 0):
            for a in ((0, 1) if d else (1,)):
                yl = p.yl if a == 0 else 1 - p.yl
                target = zs[d]
                cp = net.make(zbuf.at[j, lax.rem(p.yh + yl, 2), piece(lax.rem(target, 6))],
                              z_in.at[j, a * 8 + d], peer(yl, d))
                job["z"].append((cp, target, a * 8 + d))

                @pl.when(target < 6)
                def _(cp=cp):
                    cp.start()

    def dp_share(j):
        job = jobs[j]

        @pl.when(p.z < 6)
        def _():
            r = lax.rem(p.yh + p.yl, 2)
            t = zbuf[j, r, piece(p.z), :].astype(F32)
            for cp, _, slot in job["z"]:
                cp.wait_recv()
                t = t + z_in[j, slot].astype(F32)
            own[j] = t.astype(BF)

            @pl.when(p.yl == 0)
            def _():
                fin[j, 0, piece(p.z), :] = own[j]

        for cp, target, _ in job["z"]:
            @pl.when(target < 6)
            def _(cp=cp):
                cp.wait_send()

        job["f"] = []
        base = net.n
        net.n += 16
        for d in (4, 3, 5, 2, 6, 1, 7, 0):
            for yl in range(2):
                cp = pltpu.make_async_remote_copy(
                    src_ref=own.at[j], dst_ref=fin.at[j, p.yl, piece(lax.rem(p.z, 6))],
                    send_sem=send.at[base + yl * 8 + d], recv_sem=recv.at[base + p.yl * 8 + d],
                    device_id=peer(yl, d, lax.rem(p.yh + p.yl, 2)), device_id_type=MESH)
                source = lax.rem(p.z + (8 - d), 8)
                land = fin.at[j, yl, piece(lax.rem(source, 6))]
                arrive = pltpu.make_async_remote_copy(
                    src_ref=land, dst_ref=land, send_sem=send.at[base + yl * 8 + d],
                    recv_sem=recv.at[base + yl * 8 + d], device_id=right, device_id_type=MESH)
                real = p.z < 6
                comes = source < 6
                if d == 0 and yl == 0:
                    real = jnp.logical_and(real, p.yl == 1)
                    comes = jnp.logical_and(comes, p.yl == 1)
                job["f"].append((cp, real, arrive, comes))

                @pl.when(real)
                def _(cp=cp):
                    cp.start()

    def write(j):
        for cp, real, arrive, comes in jobs[j]["f"]:
            @pl.when(comes)
            def _(arrive=arrive):
                arrive.wait_recv()

            @pl.when(real)
            def _(cp=cp):
                cp.wait_send()

        for g in range(2):
            t = fin[j, lax.rem(p.yh + g, 2)]
            for i in range(3):
                gw[:, pl.ds(j * 2 * GW + g * GW + i * 128, 128)] = t[i * WROWS:(i + 1) * WROWS]

    def far(j):
        part_cols = pl.ds(j * GW, GW)
        return net.go(dproj.at[far_rows, part_cols], dfar.at[:, part_cols], ypair)

    fars = [far(0)]
    terms(0)
    x_first(0)
    for h in range(GROUP):
        own_k[h].wait_recv()
        lands[h].wait_recv()
        t = kpart[1, h, 1].astype(F32) + ksib[1, h].astype(F32) + kland[h].astype(F32)
        dproj[:, pl.ds(GW + h * HEAD, HEAD)] = t[:, :HEAD].astype(BF)
        dproj[:, pl.ds(2 * GW + h * HEAD, HEAD)] = t[:, HEAD:].astype(BF)
    fars += [far(1), far(2)]
    terms(1)
    terms(2)
    x_second(0)
    x_first(1)
    x_first(2)
    dp_sum(0)
    x_second(1)
    x_second(2)
    w_far.wait_recv()
    w_sib = net.go(w3.at[half_w], w3.at[half_w], sib)
    dp_share(0)
    dp_sum(1)
    part_gi = lax.dot_general(dproj[my_rows, :], w2[...], NT, preferred_element_type=F32)
    dp_sum(2)
    dp_share(1)
    w_sib.wait_recv()
    for cp in fars:
        cp.wait_recv()
    gi[...] = (part_gi + lax.dot_general(dfar[...], w3[...], NT, preferred_element_type=F32)).astype(BF)
    dp_share(2)
    write(0)
    write(1)
    write(2)
    al.wait()
    ao.wait_recv()
    net.drain()


VMEM = pl.BlockSpec(memory_space=pltpu.VMEM)


def on_device(seq_embed, w_qkv, upstream):
    scratch = [
        ((N, D), BF), ((D, GC), BF), ((2 * N, KW), BF), ((2, 2, N, KW), BF),
        ((8, 2 * N), F32), ((8, 2 * N), F32), ((GW, 2 * N), F32), ((16, 2 * N), F32), ((16, 2 * N), F32),
        ((8, 2 * N), F32), ((8, 2 * N), F32),
        ((GW, N), BF), ((GW, N), BF), ((N, GW), BF), ((GW, 2 * N), F32), ((GW, N), BF), ((GW, N), BF),
        ((2, GROUP, 2, N, 2 * HEAD), BF), ((GROUP, N, 2 * HEAD), BF), ((2, GROUP, N, 2 * HEAD), BF),
        ((GROUP, N, 2 * HEAD), BF), ((N, GC), BF),
        ((3, 4, 2, 2, WROWS, GW), BF), ((3, 3, 2, WROWS, GW), BF), ((3, 4, 2, WROWS, GW), BF),
        ((3, WROWS, GW), BF), ((3, WROWS, GW), BF), ((3, 2, WROWS, GW), BF), ((3, 2, WROWS, GW), BF),
        ((ROWS, GC), BF), ((D, GC), BF),
        ((3, 2, 288, 128), BF), ((3, 16, 48, 128), BF), ((3, 48, 128), BF), ((3, 2, 288, 128), BF),
    ]
    copies = 192
    att, gi, gw = pl.pallas_call(
        step_kernel,
        out_shape=[jax.ShapeDtypeStruct(s, BF) for s in ((ROWS, KW), (ROWS, D), (WROWS, 2 * GC))],
        in_specs=[VMEM] * 3,
        out_specs=[VMEM] * 3,
        scratch_shapes=[pltpu.VMEM(s, t) for s, t in scratch] + [
            pltpu.SemaphoreType.DMA((copies,)), pltpu.SemaphoreType.DMA((copies,)),
            pltpu.SemaphoreType.DMA((8,))],
        compiler_params=pltpu.CompilerParams(
            collective_id=0, has_side_effects=True, vmem_limit_bytes=58 * 2**20),
    )(seq_embed[0], w_qkv, upstream[0])
    return att[None], gi[None], gw


def solution(mesh):
    placed = (P("dp", "seq", None), P("seq", None), P("dp", "seq", None))
    return jax.shard_map(
        on_device,
        mesh=mesh,
        in_specs=placed,
        out_specs=(P("dp", "seq", None), P("dp", "seq", None), P("seq", None)),
        check_vma=False,
    )
```

```python
import math

import jax
import jax.numpy as jnp
from jax import lax
from jax.experimental import pallas as pl
from jax.experimental.pallas import tpu as pltpu
from jax.sharding import PartitionSpec as P

MESH = pl.DeviceIdType.MESH
BF = jnp.bfloat16
F32 = jnp.float32
ROWS = 192
D = 1536
HEAD = 128
GROUP = 3
GW = GROUP * HEAD
WROWS = 96
HALF_SCALE = 1.0 / math.sqrt(HEAD)
LOG2E = 1.4426950408889634


class Place:
    def __init__(self):
        dp, seq = lax.axis_index("dp"), lax.axis_index("seq")
        self.z, self.yl = lax.rem(dp, 8), lax.div(dp, 8)
        self.c, self.yh, self.x = lax.rem(seq, 2), lax.rem(lax.div(seq, 2), 2), lax.div(seq, 4)

    def device(self, x=None, yh=None, c=None, yl=None, z=None):
        x = self.x if x is None else x
        yh = self.yh if yh is None else yh
        c = self.c if c is None else c
        yl = self.yl if yl is None else yl
        z = self.z if z is None else z
        return (yl * 8 + z, x * 4 + yh * 2 + c)

    def xs(self, dx):
        return lax.rem(self.x + (dx + 4), 4)


class Net:
    def __init__(self, send, recv, local):
        self.send, self.recv, self.local = send, recv, local
        self.n = 0
        self.m = 0
        self.all = []

    def go(self, src, dst, device):
        cp = pltpu.make_async_remote_copy(
            src_ref=src, dst_ref=dst, send_sem=self.send.at[self.n], recv_sem=self.recv.at[self.n],
            device_id=device, device_id_type=MESH,
        )
        self.n += 1
        cp.start()
        self.all.append(cp)
        return cp

    def make(self, src, dst, device):
        self.n += 1
        return pltpu.make_async_remote_copy(
            src_ref=src, dst_ref=dst, send_sem=self.send.at[self.n - 1], recv_sem=self.recv.at[self.n - 1],
            device_id=device, device_id_type=MESH,
        )

    def here(self, src, dst):
        cp = pltpu.make_async_copy(src, dst, self.local.at[self.m])
        self.m += 1
        cp.start()
        return cp

    def drain(self):
        for cp in self.all:
            cp.wait_send()


def greet(devices):
    barrier = pltpu.get_barrier_semaphore()
    for device in devices:
        pl.semaphore_signal(barrier, inc=1, device_id=device, device_id_type=MESH)
    pl.semaphore_wait(barrier, len(devices))


def rows_of(start, size, unit):
    return pl.ds(pl.multiple_of(start, unit), size)


NT = (((1,), (1,)), ((), ()))
TN = (((0,), (0,)), ((), ()))
N = 2 * ROWS
GC = 3 * GW
KW = 2 * GW


def step_kernel(x_ref, w_ref, g_ref, att, gi, gw,
                x2, w2, qg, kv, m_ref, l_ref, o_ref, stat_out, stat_in, lse_ref, delta_ref,
                o_out, o_in, o2, dq_ref, dq_out, dq_in, kpart, kother, ksib, kland, dproj,
                part, other, sibl, land_a, land_b, land_l, land_r,
                dfar, w3, zbuf, z_in, own, fin, send, recv, local):
    p = Place()
    net = Net(send, recv, local)
    ypair = p.device(yh=1 - p.yh)
    mirror = p.device(yh=1 - p.yh, yl=1 - p.yl)
    near = p.device(yl=1 - p.yl)
    right, left, sib = p.device(x=p.xs(1)), p.device(x=p.xs(-1)), p.device(c=1 - p.c)
    odd = lax.rem(p.x, 2)
    qpair, kpair = p.device(x=p.xs(1 - 2 * odd)), p.device(x=p.xs(2 * odd - 1))
    zs = [lax.rem(p.z + d, 8) for d in range(8)]

    def wrows(x, yh):
        return w2.at[rows_of((x * 4 + yh * 2 + p.c) * WROWS, WROWS, 32)]

    def wcols(yh, j):
        return w_ref.at[:, rows_of(yh * GW + 2 * GW * j, GW, 128)]

    mine = wrows(p.x, p.yh)
    my_rows = rows_of(p.yh * ROWS, ROWS, 64)
    far_rows = rows_of((1 - p.yh) * ROWS, ROWS, 64)
    own_w = [net.here(wcols(p.yh, j), mine.at[:, pl.ds(j * GW, GW)]) for j in range(3)]
    own_x = net.here(x_ref, x2.at[my_rows])
    own_g = net.here(g_ref.at[:, rows_of(p.yh * GW, GW, 128)], qg.at[my_rows, pl.ds(GW, GW)])
    greet([right, left, sib] + [
        p.device(yh=p.yh if a == 0 else 1 - p.yh, yl=p.yl if b == 0 else 1 - p.yl, z=zs[d])
        for d in range(8) for a in range(2) for b in range(2) if d + a + b > 0])
    theirs = [net.go(wcols(1 - p.yh, j), mine.at[:, pl.ds(j * GW, GW)], mirror) for j in range(3)]
    for cp in own_w:
        cp.wait()
    a_right, a_left = net.go(mine, mine, right), net.go(mine, mine, left)
    relays = [net.go(mine, mine, sib)]

    def relay(x, yh):
        block = wrows(x, yh)
        relays.append(net.go(block, block, sib))

    own_x.wait()
    own_g.wait()
    for cp in theirs:
        cp.wait_recv()
    mine_x = x2.at[my_rows]
    xo = net.go(mine_x, mine_x, ypair)
    block = wrows(p.x, 1 - p.yh)
    b_right, b_left = net.go(block, block, right), net.go(block, block, left)
    relay(p.x, 1 - p.yh)
    a_right.wait_recv()
    block = wrows(p.xs(-1), p.yh)
    f_right = net.go(block, block, right)
    relay(p.xs(-1), p.yh)
    a_left.wait_recv()
    relay(p.xs(1), p.yh)
    b_left.wait_recv()
    block = wrows(p.xs(1), 1 - p.yh)
    f_left = net.go(block, block, left)
    relay(p.xs(1), 1 - p.yh)
    b_right.wait_recv()
    relay(p.xs(-1), 1 - p.yh)
    go = net.go(g_ref.at[:, rows_of((1 - p.yh) * GW, GW, 128)], qg.at[my_rows, pl.ds(GW, GW)], ypair)
    f_right.wait_recv()
    relay(p.xs(2), p.yh)
    f_left.wait_recv()
    relay(p.xs(2), 1 - p.yh)
    for cp in relays:
        cp.wait_recv()

    half_w = rows_of(p.c * (D // 2), D // 2, 256)

    def project(tokens, rows, j):
        t = jnp.dot(tokens[...], w2[:, pl.ds(j * GW, GW)], preferred_element_type=F32).astype(BF)
        if j == 0:
            qg[rows, pl.ds(0, GW)] = t
        else:
            kv[0, p.c, rows, pl.ds((j - 1) * GW, GW)] = t

    def give(rows):
        mk, mq = kv.at[0, p.c, rows], qg.at[rows, pl.ds(0, GW)]
        out = [net.go(mk, kv.at[1, p.c, rows], kpair), net.go(mk, mk, sib)]
        return out, mq

    project(mine_x, my_rows, 1)
    project(mine_x, my_rows, 2)
    (k_a, s_a), mq = give(my_rows)
    project(mine_x, my_rows, 0)
    there = rows_of(N + p.yh * ROWS, ROWS, 64)
    q_a = net.go(mq, qg.at[there, pl.ds(0, GW)], qpair)
    xo.wait_recv()
    far_x = x2.at[far_rows]
    project(far_x, far_rows, 1)
    project(far_x, far_rows, 2)
    (k_b, s_b), mq = give(far_rows)
    project(far_x, far_rows, 0)
    there_b = rows_of(N + (1 - p.yh) * ROWS, ROWS, 64)
    q_b = net.go(mq, qg.at[there_b, pl.ds(0, GW)], qpair)
    g_cols = pl.ds(GW, GW)
    g_a = net.go(qg.at[my_rows, g_cols], qg.at[there, g_cols], qpair)
    go.wait_recv()
    g_b = net.go(qg.at[far_rows, g_cols], qg.at[there_b, g_cols], qpair)
    w_far = net.go(w2.at[half_w], w3.at[half_w], mirror)

    m_ref[...] = jnp.full_like(m_ref, -1e30)
    l_ref[...] = jnp.zeros_like(l_ref)
    o_ref[...] = jnp.zeros_like(o_ref)
    c2 = HALF_SCALE * LOG2E

    def forward(b, rows, lo, size, core=None):
        qr = pl.ds(lo, size)
        for h in range(GROUP):
            q = qg[qr, pl.ds(h * HEAD, HEAD)]
            k_cols, v_cols = pl.ds(h * HEAD, HEAD), pl.ds(GW + h * HEAD, HEAD)
            if core is None:
                keys, values = kv[b, :, rows, k_cols].reshape(N, HEAD), kv[b, :, rows, v_cols].reshape(N, HEAD)
            else:
                keys, values = kv[b, core, rows, k_cols], kv[b, core, rows, v_cols]
            s = lax.dot_general(keys, q, NT, preferred_element_type=F32) * c2
            hs, hr = pl.ds(h, 1), pl.ds(h * HEAD, HEAD)
            m_old = m_ref[hs, qr]
            m_new = jnp.maximum(m_old, jnp.max(s, axis=0, keepdims=True))
            alpha = jnp.exp2(m_old - m_new)
            e = jnp.exp2(s - m_new)
            m_ref[hs, qr] = m_new
            l_ref[hs, qr] = l_ref[hs, qr] * alpha + jnp.sum(e, axis=0, keepdims=True)
            o_ref[hr, qr] = o_ref[hr, qr] * alpha + jnp.dot(
                values.T, e.astype(BF), preferred_element_type=F32)

    s_a.wait_recv()
    forward(0, my_rows, 0, N)
    s_b.wait_recv()
    forward(0, far_rows, 0, N)
    k_a.wait_recv()
    t_a = net.go(kv.at[1, p.c, my_rows], kv.at[1, p.c, my_rows], sib)
    t_a.wait_recv()
    forward(1, my_rows, 0, N)
    q_a.wait_recv()
    q_b.wait_recv()
    forward(0, my_rows, N, N)
    forward(0, far_rows, N, N)
    forward(1, my_rows, N, N)
    k_b.wait_recv()
    t_b = net.go(kv.at[1, p.c, far_rows], kv.at[1, p.c, far_rows], sib)
    forward(1, far_rows, 0, 2 * N, p.c)
    t_b.wait_recv()
    forward(1, far_rows, 0, 2 * N, 1 - p.c)
    g_a.wait_recv()
    g_b.wait_recv()

    stat_out[...] = jnp.zeros_like(stat_out)
    for h in range(GROUP):
        hr = pl.ds(h * HEAD, HEAD)
        stat_out[pl.ds(h, 1), :] = m_ref[pl.ds(h, 1), :]
        stat_out[pl.ds(GROUP + h, 1), :] = l_ref[pl.ds(h, 1), :]
        stat_out[pl.ds(2 * GROUP + h, 1), :] = jnp.sum(
            o_ref[hr, :] * qg[:, pl.ds(GW + h * HEAD, HEAD)].T.astype(F32), axis=0, keepdims=True)
    st = net.go(stat_out, stat_in, qpair)
    st.wait_recv()

    def stat(i):
        other_half = stat_in[pl.ds(i, 1), :]
        return stat_out[pl.ds(i, 1), :], jnp.concatenate([other_half[:, N:], other_half[:, :N]], axis=1)

    for h in range(GROUP):
        hs = pl.ds(h, 1)
        m1, m2 = stat(h)
        l1, l2 = stat(GROUP + h)
        d1, d2 = stat(2 * GROUP + h)
        m = jnp.maximum(m1, m2)
        f1, f2 = jnp.exp2(m1 - m), jnp.exp2(m2 - m)
        l = l1 * f1 + l2 * f2
        lse_ref[hs, :] = m + jnp.log2(l)
        delta_ref[hs, :] = (d1 * f1 + d2 * f2) / l
        l_ref[hs, :] = f1 / l
    dq_ref[...] = jnp.zeros_like(dq_ref)

    def backward(i, b, h, own_core):
        hr = pl.ds(h * HEAD, HEAD)
        c = p.c if own_core else 1 - p.c
        q, g = qg[:, hr], qg[:, pl.ds(GW + h * HEAD, HEAD)]
        k = kv[b, c, :, hr]
        s = lax.dot_general(k, q, NT, preferred_element_type=F32) * c2
        e = jnp.exp2(s - lse_ref[pl.ds(h, 1), :])
        dv = jnp.dot(e.astype(BF), g, preferred_element_type=F32).astype(BF)
        de = lax.dot_general(kv[b, c, :, pl.ds(GW + h * HEAD, HEAD)], g, NT, preferred_element_type=F32)
        ds = (e * (de - delta_ref[pl.ds(h, 1), :])).astype(BF)
        dk = (jnp.dot(ds, q, preferred_element_type=F32) * HALF_SCALE).astype(BF)
        dq_ref[hr, :] += jnp.dot(k.T, ds, preferred_element_type=F32)
        kpart[i, h, own_core, :, pl.ds(0, HEAD)] = dk
        kpart[i, h, own_core, :, pl.ds(HEAD, HEAD)] = dv
        return None if own_core else net.go(kpart.at[i, h, 0], ksib.at[i, h], sib)

    for h in range(GROUP):
        hr = pl.ds(h * HEAD, HEAD)
        o_ref[hr, :] = o_ref[hr, :] * l_ref[pl.ds(h, 1), :]
        o_out[hr, :] = o_ref[hr, pl.ds(N, N)].astype(BF)
    oc = net.go(o_out, o_in, qpair)
    lands = []
    for h in range(GROUP):
        cp = backward(0, 1, h, 0)
        backward(0, 1, h, 1)
        cp.wait_recv()
        kother[h] = (kpart[0, h, 1].astype(F32) + ksib[0, h].astype(F32)).astype(BF)
        lands.append(net.go(kother.at[h], kland.at[h], kpair))
    own_k, dqs = [], []
    for h in range(GROUP):
        hr = pl.ds(h * HEAD, HEAD)
        own_k.append(backward(1, 0, h, 0))
        backward(1, 0, h, 1)
        dq_out[hr, :] = (dq_ref[hr, pl.ds(N, N)] * HALF_SCALE).astype(BF)
        dqs.append(net.go(dq_out.at[hr], dq_in.at[hr], qpair))
    oc.wait_recv()
    for h in range(GROUP):
        hr = pl.ds(h * HEAD, HEAD)
        o2[:, hr] = (o_ref[hr, pl.ds(0, N)] + o_in[hr, :].astype(F32)).astype(BF).T
    cols = rows_of(p.yh * GW, GW, 128)
    ao = net.go(o2.at[far_rows], att.at[:, cols], ypair)
    al = net.here(o2.at[my_rows], att.at[:, cols])
    for h in range(GROUP):
        hr = pl.ds(h * HEAD, HEAD)
        dqs[h].wait_recv()
        dproj[:, hr] = (dq_ref[hr, pl.ds(0, N)] * HALF_SCALE + dq_in[hr, :].astype(F32)).astype(BF).T

    order = [p.xs(2), p.xs(1), p.xs(-1), p.x]
    jobs = [{"sib": []} for _ in range(3)]

    def terms(j, blocks):
        for i in blocks:
            x = order[i]
            t = lax.dot_general(x2[:, rows_of(x * GW, GW, 128)], dproj[:, pl.ds(j * GW, GW)], TN,
                                preferred_element_type=F32).astype(BF)
            for c in range(2):
                for yh in range(2):
                    lo = (yh * 2 + c) * WROWS
                    part[j, i, c, yh] = t[lo:lo + WROWS]
            jobs[j]["sib"].append(net.go(part.at[j, i, 1 - p.c], sibl.at[j, i], sib))

    def add(j, i, yh, *lands):
        t = part[j, i, p.c, yh].astype(F32) + sibl[j, i, yh].astype(F32)
        for ref in lands:
            t = t + ref.astype(F32)
        return t

    def x_first(j):
        jobs[j]["sib"][0].wait_recv()
        for yh in range(2):
            other[j, 0, yh] = add(j, 0, yh).astype(BF)
        jobs[j]["a"] = net.go(other.at[j, 0, 0], land_a.at[j], right)
        jobs[j]["b"] = net.go(other.at[j, 0, 1], land_b.at[j], left)

    def x_second(j):
        job = jobs[j]
        job["sib"][1].wait_recv()
        job["sib"][2].wait_recv()
        other[j, 1, 1] = add(j, 1, 1).astype(BF)
        other[j, 2, 0] = add(j, 2, 0).astype(BF)
        job["a"].wait_recv()
        other[j, 1, 0] = add(j, 1, 0, land_a[j]).astype(BF)
        job["l"] = net.go(other.at[j, 1], land_l.at[j], right)
        job["b"].wait_recv()
        other[j, 2, 1] = add(j, 2, 1, land_b[j]).astype(BF)
        job["r"] = net.go(other.at[j, 2], land_r.at[j], left)

    def peer(yl, d, yh=None):
        return p.device(yh=yh, yl=yl, z=zs[d])

    def piece(z):
        return rows_of(z * 48, 48, 16)

    def dp_sum(j):
        job = jobs[j]
        job["sib"][3].wait_recv()
        job["l"].wait_recv()
        job["r"].wait_recv()
        for r in range(2):
            t = add(j, 3, r, land_l[j, r], land_r[j, r]).astype(BF)
            for i in range(3):
                zbuf[j, r, pl.ds(i * WROWS, WROWS), :] = t[:, i * 128:(i + 1) * 128]
        job["z"] = []
        for d in (4, 3, 5, 2, 6, 1, 7, 0):
            for a in ((0, 1) if d else (1,)):
                yl = p.yl if a == 0 else 1 - p.yl
                target = zs[d]
                cp = net.make(zbuf.at[j, lax.rem(p.yh + yl, 2), piece(lax.rem(target, 6))],
                              z_in.at[j, a * 8 + d], peer(yl, d))
                job["z"].append((cp, target, a * 8 + d))

                @pl.when(target < 6)
                def _(cp=cp):
                    cp.start()

    def dp_share(j):
        job = jobs[j]

        @pl.when(p.z < 6)
        def _():
            r = lax.rem(p.yh + p.yl, 2)
            t = zbuf[j, r, piece(p.z), :].astype(F32)
            for cp, _, slot in job["z"]:
                cp.wait_recv()
                t = t + z_in[j, slot].astype(F32)
            own[j] = t.astype(BF)

            @pl.when(p.yl == 0)
            def _():
                fin[j, 0, piece(p.z), :] = own[j]

        for cp, target, _ in job["z"]:
            @pl.when(target < 6)
            def _(cp=cp):
                cp.wait_send()

        job["f"] = []
        base = net.n
        net.n += 16
        for d in (4, 3, 5, 2, 6, 1, 7, 0):
            for yl in range(2):
                cp = pltpu.make_async_remote_copy(
                    src_ref=own.at[j], dst_ref=fin.at[j, p.yl, piece(lax.rem(p.z, 6))],
                    send_sem=send.at[base + yl * 8 + d], recv_sem=recv.at[base + p.yl * 8 + d],
                    device_id=peer(yl, d, lax.rem(p.yh + p.yl, 2)), device_id_type=MESH)
                source = lax.rem(p.z + (8 - d), 8)
                land = fin.at[j, yl, piece(lax.rem(source, 6))]
                arrive = pltpu.make_async_remote_copy(
                    src_ref=land, dst_ref=land, send_sem=send.at[base + yl * 8 + d],
                    recv_sem=recv.at[base + yl * 8 + d], device_id=right, device_id_type=MESH)
                real = p.z < 6
                comes = source < 6
                if d == 0 and yl == 0:
                    real = jnp.logical_and(real, p.yl == 1)
                    comes = jnp.logical_and(comes, p.yl == 1)
                job["f"].append((cp, real, arrive, comes))

                @pl.when(real)
                def _(cp=cp):
                    cp.start()

    def write(j):
        for cp, real, arrive, comes in jobs[j]["f"]:
            @pl.when(comes)
            def _(arrive=arrive):
                arrive.wait_recv()

            @pl.when(real)
            def _(cp=cp):
                cp.wait_send()

        for g in range(2):
            t = fin[j, lax.rem(p.yh + g, 2)]
            for i in range(3):
                gw[:, pl.ds(j * 2 * GW + g * GW + i * 128, 128)] = t[i * WROWS:(i + 1) * WROWS]

    def far(j):
        part_cols = pl.ds(j * GW, GW)
        return net.go(dproj.at[far_rows, part_cols], dfar.at[:, part_cols], ypair)

    fars = [far(0)]
    terms(0, (0,))
    terms(0, (1, 2, 3))
    x_first(0)
    for h in range(GROUP):
        own_k[h].wait_recv()
        lands[h].wait_recv()
        t = kpart[1, h, 1].astype(F32) + ksib[1, h].astype(F32) + kland[h].astype(F32)
        dproj[:, pl.ds(GW + h * HEAD, HEAD)] = t[:, :HEAD].astype(BF)
        dproj[:, pl.ds(2 * GW + h * HEAD, HEAD)] = t[:, HEAD:].astype(BF)
    fars += [far(1), far(2)]
    terms(1, (0,))
    terms(2, (0,))
    x_second(0)
    x_first(1)
    x_first(2)
    terms(1, (1, 2))
    terms(2, (1, 2))
    dp_sum(0)
    x_second(1)
    x_second(2)
    terms(1, (3,))
    terms(2, (3,))
    w_far.wait_recv()
    w_sib = net.go(w3.at[half_w], w3.at[half_w], sib)
    dp_share(0)
    dp_sum(1)
    part_gi = lax.dot_general(dproj[my_rows, :], w2[...], NT, preferred_element_type=F32)
    dp_sum(2)
    dp_share(1)
    dp_share(2)
    w_sib.wait_recv()
    for cp in fars:
        cp.wait_recv()
    gi[...] = (part_gi + lax.dot_general(dfar[...], w3[...], NT, preferred_element_type=F32)).astype(BF)
    write(0)
    write(1)
    write(2)
    al.wait()
    ao.wait_recv()
    net.drain()


def copy_kernel(att, gi, gw, att_out, gi_out, gw_out, a, b, c, sems):
    jobs = ((att, a, att_out.at[0]), (gi, b, gi_out.at[0]), (gw, c, gw_out))
    into = [pltpu.make_async_copy(src, mid, sems.at[i]) for i, (src, mid, _) in enumerate(jobs)]
    back = [pltpu.make_async_copy(mid, dst, sems.at[3 + i]) for i, (_, mid, dst) in enumerate(jobs)]
    for cp in into:
        cp.start()
    for x, y in zip(into, back):
        x.wait()
        y.start()
    for cp in back:
        cp.wait()


VMEM = pl.BlockSpec(memory_space=pltpu.VMEM)
ANY = pl.BlockSpec(memory_space=pl.ANY)


def on_device(seq_embed, w_qkv, upstream):
    scratch = [
        ((N, D), BF), ((D, GC), BF), ((2 * N, KW), BF), ((2, 2, N, KW), BF),
        ((8, 2 * N), F32), ((8, 2 * N), F32), ((GW, 2 * N), F32), ((16, 2 * N), F32), ((16, 2 * N), F32),
        ((8, 2 * N), F32), ((8, 2 * N), F32),
        ((GW, N), BF), ((GW, N), BF), ((N, GW), BF), ((GW, 2 * N), F32), ((GW, N), BF), ((GW, N), BF),
        ((2, GROUP, 2, N, 2 * HEAD), BF), ((GROUP, N, 2 * HEAD), BF), ((2, GROUP, N, 2 * HEAD), BF),
        ((GROUP, N, 2 * HEAD), BF), ((N, GC), BF),
        ((3, 4, 2, 2, WROWS, GW), BF), ((3, 3, 2, WROWS, GW), BF), ((3, 4, 2, WROWS, GW), BF),
        ((3, WROWS, GW), BF), ((3, WROWS, GW), BF), ((3, 2, WROWS, GW), BF), ((3, 2, WROWS, GW), BF),
        ((ROWS, GC), BF), ((D, GC), BF),
        ((3, 2, 288, 128), BF), ((3, 16, 48, 128), BF), ((3, 48, 128), BF), ((3, 2, 288, 128), BF),
    ]
    copies = 192
    att, gi, gw = pl.pallas_call(
        step_kernel,
        out_shape=[jax.ShapeDtypeStruct(s, BF) for s in ((ROWS, KW), (ROWS, D), (WROWS, 2 * GC))],
        in_specs=[ANY] * 3,
        out_specs=[VMEM] * 3,
        scratch_shapes=[pltpu.VMEM(s, t) for s, t in scratch] + [
            pltpu.SemaphoreType.DMA((copies,)), pltpu.SemaphoreType.DMA((copies,)),
            pltpu.SemaphoreType.DMA((8,))],
        compiler_params=pltpu.CompilerParams(
            collective_id=0, has_side_effects=True, vmem_limit_bytes=58 * 2**20),
    )(seq_embed[0], w_qkv, upstream[0])
    return pl.pallas_call(
        copy_kernel,
        out_shape=[jax.ShapeDtypeStruct(s, BF) for s in ((1, ROWS, KW), (1, ROWS, D), (WROWS, 2 * GC))],
        in_specs=[ANY] * 3,
        out_specs=[ANY] * 3,
        scratch_shapes=[pltpu.VMEM(s, BF) for s in ((ROWS, KW), (ROWS, D), (WROWS, 2 * GC))] + [
            pltpu.SemaphoreType.DMA((6,))],
    )(att, gi, gw)


def solution(mesh):
    placed = (P("dp", "seq", None), P("seq", None), P("dp", "seq", None))
    return jax.shard_map(
        on_device,
        mesh=mesh,
        in_specs=placed,
        out_specs=(P("dp", "seq", None), P("dp", "seq", None), P("seq", None)),
        check_vma=False,
    )
```

```python
import math

import jax
import jax.numpy as jnp
from jax import lax
from jax.experimental import pallas as pl
from jax.experimental.pallas import tpu as pltpu
from jax.sharding import PartitionSpec as P

MESH = pl.DeviceIdType.MESH
BF = jnp.bfloat16
F32 = jnp.float32
ROWS = 192
D = 1536
HEAD = 128
GROUP = 3
GW = GROUP * HEAD
WROWS = 96
HALF_SCALE = 1.0 / math.sqrt(HEAD)
LOG2E = 1.4426950408889634


class Place:
    def __init__(self):
        dp, seq = lax.axis_index("dp"), lax.axis_index("seq")
        self.z, self.yl = lax.rem(dp, 8), lax.div(dp, 8)
        self.c, self.yh, self.x = lax.rem(seq, 2), lax.rem(lax.div(seq, 2), 2), lax.div(seq, 4)

    def device(self, x=None, yh=None, c=None, yl=None, z=None):
        x = self.x if x is None else x
        yh = self.yh if yh is None else yh
        c = self.c if c is None else c
        yl = self.yl if yl is None else yl
        z = self.z if z is None else z
        return (yl * 8 + z, x * 4 + yh * 2 + c)

    def xs(self, dx):
        return lax.rem(self.x + (dx + 4), 4)


class Net:
    def __init__(self, send, recv, local):
        self.send, self.recv, self.local = send, recv, local
        self.n = 0
        self.m = 0
        self.all = []

    def go(self, src, dst, device):
        cp = pltpu.make_async_remote_copy(
            src_ref=src, dst_ref=dst, send_sem=self.send.at[self.n], recv_sem=self.recv.at[self.n],
            device_id=device, device_id_type=MESH,
        )
        self.n += 1
        cp.start()
        self.all.append(cp)
        return cp

    def make(self, src, dst, device):
        self.n += 1
        return pltpu.make_async_remote_copy(
            src_ref=src, dst_ref=dst, send_sem=self.send.at[self.n - 1], recv_sem=self.recv.at[self.n - 1],
            device_id=device, device_id_type=MESH,
        )

    def here(self, src, dst):
        cp = pltpu.make_async_copy(src, dst, self.local.at[self.m])
        self.m += 1
        cp.start()
        return cp

    def drain(self):
        for cp in self.all:
            cp.wait_send()


def greet(devices):
    barrier = pltpu.get_barrier_semaphore()
    for device in devices:
        pl.semaphore_signal(barrier, inc=1, device_id=device, device_id_type=MESH)
    pl.semaphore_wait(barrier, len(devices))


def rows_of(start, size, unit):
    return pl.ds(pl.multiple_of(start, unit), size)


NT = (((1,), (1,)), ((), ()))
TN = (((0,), (0,)), ((), ()))
N = 2 * ROWS
GC = 3 * GW
KW = 2 * GW


def step_kernel(x_ref, w_ref, g_ref, att, gi, gw,
                x2, w2, qg, kv, m_ref, l_ref, o_ref, stat_out, stat_in, lse_ref, delta_ref,
                o_out, o_in, o2, dq_ref, dq_out, dq_in, kpart, kother, ksib, kland, dproj,
                part, other, sibl, land_a, land_b, land_l, land_r,
                dfar, w3, zbuf, z_in, own, fin, send, recv, local):
    p = Place()
    net = Net(send, recv, local)
    ypair = p.device(yh=1 - p.yh)
    mirror = p.device(yh=1 - p.yh, yl=1 - p.yl)
    near = p.device(yl=1 - p.yl)
    right, left, sib = p.device(x=p.xs(1)), p.device(x=p.xs(-1)), p.device(c=1 - p.c)
    odd = lax.rem(p.x, 2)
    qpair, kpair = p.device(x=p.xs(1 - 2 * odd)), p.device(x=p.xs(2 * odd - 1))
    zs = [lax.rem(p.z + d, 8) for d in range(8)]

    def wrows(x, yh):
        return w2.at[rows_of((x * 4 + yh * 2 + p.c) * WROWS, WROWS, 32)]

    def wcols(yh, j):
        return w_ref.at[:, rows_of(yh * GW + 2 * GW * j, GW, 128)]

    mine = wrows(p.x, p.yh)
    my_rows = rows_of(p.yh * ROWS, ROWS, 64)
    far_rows = rows_of((1 - p.yh) * ROWS, ROWS, 64)
    own_w = [net.here(wcols(p.yh, j), mine.at[:, pl.ds(j * GW, GW)]) for j in range(3)]
    own_x = net.here(x_ref, x2.at[my_rows])
    own_g = net.here(g_ref.at[:, rows_of(p.yh * GW, GW, 128)], qg.at[my_rows, pl.ds(GW, GW)])
    greet([right, left, sib] + [
        p.device(yh=p.yh if a == 0 else 1 - p.yh, yl=p.yl if b == 0 else 1 - p.yl, z=zs[d])
        for d in range(8) for a in range(2) for b in range(2) if d + a + b > 0])
    theirs = [net.go(wcols(1 - p.yh, j), mine.at[:, pl.ds(j * GW, GW)], mirror) for j in range(3)]
    for cp in own_w:
        cp.wait()
    a_right, a_left = net.go(mine, mine, right), net.go(mine, mine, left)
    relays = [net.go(mine, mine, sib)]

    def relay(x, yh):
        block = wrows(x, yh)
        relays.append(net.go(block, block, sib))

    own_x.wait()
    own_g.wait()
    for cp in theirs:
        cp.wait_recv()
    mine_x = x2.at[my_rows]
    xo = net.go(mine_x, mine_x, ypair)
    block = wrows(p.x, 1 - p.yh)
    b_right, b_left = net.go(block, block, right), net.go(block, block, left)
    relay(p.x, 1 - p.yh)
    a_right.wait_recv()
    block = wrows(p.xs(-1), p.yh)
    f_right = net.go(block, block, right)
    relay(p.xs(-1), p.yh)
    a_left.wait_recv()
    relay(p.xs(1), p.yh)
    b_left.wait_recv()
    block = wrows(p.xs(1), 1 - p.yh)
    f_left = net.go(block, block, left)
    relay(p.xs(1), 1 - p.yh)
    b_right.wait_recv()
    relay(p.xs(-1), 1 - p.yh)
    go = net.go(g_ref.at[:, rows_of((1 - p.yh) * GW, GW, 128)], qg.at[my_rows, pl.ds(GW, GW)], ypair)
    f_right.wait_recv()
    relay(p.xs(2), p.yh)
    f_left.wait_recv()
    relay(p.xs(2), 1 - p.yh)
    for cp in relays:
        cp.wait_recv()

    half_w = rows_of(p.c * (D // 2), D // 2, 256)

    def project(tokens, rows, j):
        t = jnp.dot(tokens[...], w2[:, pl.ds(j * GW, GW)], preferred_element_type=F32).astype(BF)
        if j == 0:
            qg[rows, pl.ds(0, GW)] = t
        else:
            kv[0, p.c, rows, pl.ds((j - 1) * GW, GW)] = t

    def give(rows):
        mk, mq = kv.at[0, p.c, rows], qg.at[rows, pl.ds(0, GW)]
        out = [net.go(mk, kv.at[1, p.c, rows], kpair), net.go(mk, mk, sib)]
        return out, mq

    project(mine_x, my_rows, 1)
    project(mine_x, my_rows, 2)
    (k_a, s_a), mq = give(my_rows)
    project(mine_x, my_rows, 0)
    there = rows_of(N + p.yh * ROWS, ROWS, 64)
    q_a = net.go(mq, qg.at[there, pl.ds(0, GW)], qpair)
    xo.wait_recv()
    far_x = x2.at[far_rows]
    project(far_x, far_rows, 1)
    project(far_x, far_rows, 2)
    (k_b, s_b), mq = give(far_rows)
    project(far_x, far_rows, 0)
    there_b = rows_of(N + (1 - p.yh) * ROWS, ROWS, 64)
    q_b = net.go(mq, qg.at[there_b, pl.ds(0, GW)], qpair)
    g_cols = pl.ds(GW, GW)
    g_a = net.go(qg.at[my_rows, g_cols], qg.at[there, g_cols], qpair)
    go.wait_recv()
    g_b = net.go(qg.at[far_rows, g_cols], qg.at[there_b, g_cols], qpair)
    w_far = net.go(w2.at[half_w], w3.at[half_w], mirror)

    m_ref[...] = jnp.full_like(m_ref, -1e30)
    l_ref[...] = jnp.zeros_like(l_ref)
    o_ref[...] = jnp.zeros_like(o_ref)
    c2 = HALF_SCALE * LOG2E

    def forward(b, rows, lo, size, core=None):
        qr = pl.ds(lo, size)
        for h in range(GROUP):
            q = qg[qr, pl.ds(h * HEAD, HEAD)]
            k_cols, v_cols = pl.ds(h * HEAD, HEAD), pl.ds(GW + h * HEAD, HEAD)
            if core is None:
                keys, values = kv[b, :, rows, k_cols].reshape(N, HEAD), kv[b, :, rows, v_cols].reshape(N, HEAD)
            else:
                keys, values = kv[b, core, rows, k_cols], kv[b, core, rows, v_cols]
            s = lax.dot_general(keys, q, NT, preferred_element_type=F32) * c2
            hs, hr = pl.ds(h, 1), pl.ds(h * HEAD, HEAD)
            m_old = m_ref[hs, qr]
            m_new = jnp.maximum(m_old, jnp.max(s, axis=0, keepdims=True))
            alpha = jnp.exp2(m_old - m_new)
            e = jnp.exp2(s - m_new)
            m_ref[hs, qr] = m_new
            l_ref[hs, qr] = l_ref[hs, qr] * alpha + jnp.sum(e, axis=0, keepdims=True)
            o_ref[hr, qr] = o_ref[hr, qr] * alpha + jnp.dot(
                values.T, e.astype(BF), preferred_element_type=F32)

    s_a.wait_recv()
    forward(0, my_rows, 0, N)
    s_b.wait_recv()
    forward(0, far_rows, 0, N)
    k_a.wait_recv()
    t_a = net.go(kv.at[1, p.c, my_rows], kv.at[1, p.c, my_rows], sib)
    t_a.wait_recv()
    forward(1, my_rows, 0, N)
    q_a.wait_recv()
    q_b.wait_recv()
    forward(0, my_rows, N, N)
    forward(0, far_rows, N, N)
    forward(1, my_rows, N, N)
    k_b.wait_recv()
    t_b = net.go(kv.at[1, p.c, far_rows], kv.at[1, p.c, far_rows], sib)
    forward(1, far_rows, 0, 2 * N, p.c)
    t_b.wait_recv()
    forward(1, far_rows, 0, 2 * N, 1 - p.c)
    g_a.wait_recv()
    g_b.wait_recv()

    stat_out[...] = jnp.zeros_like(stat_out)
    for h in range(GROUP):
        hr = pl.ds(h * HEAD, HEAD)
        stat_out[pl.ds(h, 1), :] = m_ref[pl.ds(h, 1), :]
        stat_out[pl.ds(GROUP + h, 1), :] = l_ref[pl.ds(h, 1), :]
        stat_out[pl.ds(2 * GROUP + h, 1), :] = jnp.sum(
            o_ref[hr, :] * qg[:, pl.ds(GW + h * HEAD, HEAD)].T.astype(F32), axis=0, keepdims=True)
    st = net.go(stat_out, stat_in, qpair)
    st.wait_recv()

    def stat(i):
        other_half = stat_in[pl.ds(i, 1), :]
        return stat_out[pl.ds(i, 1), :], jnp.concatenate([other_half[:, N:], other_half[:, :N]], axis=1)

    for h in range(GROUP):
        hs = pl.ds(h, 1)
        m1, m2 = stat(h)
        l1, l2 = stat(GROUP + h)
        d1, d2 = stat(2 * GROUP + h)
        m = jnp.maximum(m1, m2)
        f1, f2 = jnp.exp2(m1 - m), jnp.exp2(m2 - m)
        l = l1 * f1 + l2 * f2
        lse_ref[hs, :] = m + jnp.log2(l)
        delta_ref[hs, :] = (d1 * f1 + d2 * f2) / l
        l_ref[hs, :] = f1 / l
    dq_ref[...] = jnp.zeros_like(dq_ref)

    def backward(i, b, h, own_core):
        hr = pl.ds(h * HEAD, HEAD)
        c = p.c if own_core else 1 - p.c
        q, g = qg[:, hr], qg[:, pl.ds(GW + h * HEAD, HEAD)]
        k = kv[b, c, :, hr]
        s = lax.dot_general(k, q, NT, preferred_element_type=F32) * c2
        e = jnp.exp2(s - lse_ref[pl.ds(h, 1), :])
        dv = jnp.dot(e.astype(BF), g, preferred_element_type=F32).astype(BF)
        de = lax.dot_general(kv[b, c, :, pl.ds(GW + h * HEAD, HEAD)], g, NT, preferred_element_type=F32)
        ds = (e * (de - delta_ref[pl.ds(h, 1), :])).astype(BF)
        dk = (jnp.dot(ds, q, preferred_element_type=F32) * HALF_SCALE).astype(BF)
        dq_ref[hr, :] += jnp.dot(k.T, ds, preferred_element_type=F32)
        kpart[i, h, own_core, :, pl.ds(0, HEAD)] = dk
        kpart[i, h, own_core, :, pl.ds(HEAD, HEAD)] = dv
        return None if own_core else net.go(kpart.at[i, h, 0], ksib.at[i, h], sib)

    for h in range(GROUP):
        hr = pl.ds(h * HEAD, HEAD)
        o_ref[hr, :] = o_ref[hr, :] * l_ref[pl.ds(h, 1), :]
        o_out[hr, :] = o_ref[hr, pl.ds(N, N)].astype(BF)
    oc = net.go(o_out, o_in, qpair)
    lands = []
    for h in range(GROUP):
        cp = backward(0, 1, h, 0)
        backward(0, 1, h, 1)
        cp.wait_recv()
        kother[h] = (kpart[0, h, 1].astype(F32) + ksib[0, h].astype(F32)).astype(BF)
        lands.append(net.go(kother.at[h], kland.at[h], kpair))
    own_k, dqs = [], []
    for h in range(GROUP):
        hr = pl.ds(h * HEAD, HEAD)
        own_k.append(backward(1, 0, h, 0))
        backward(1, 0, h, 1)
        dq_out[hr, :] = (dq_ref[hr, pl.ds(N, N)] * HALF_SCALE).astype(BF)
        dqs.append(net.go(dq_out.at[hr], dq_in.at[hr], qpair))
    oc.wait_recv()
    for h in range(GROUP):
        hr = pl.ds(h * HEAD, HEAD)
        o2[:, hr] = (o_ref[hr, pl.ds(0, N)] + o_in[hr, :].astype(F32)).astype(BF).T
    cols = rows_of(p.yh * GW, GW, 128)
    ao = net.go(o2.at[far_rows], att.at[:, cols], ypair)
    al = net.here(o2.at[my_rows], att.at[:, cols])
    for h in range(GROUP):
        hr = pl.ds(h * HEAD, HEAD)
        dqs[h].wait_recv()
        dproj[:, hr] = (dq_ref[hr, pl.ds(0, N)] * HALF_SCALE + dq_in[hr, :].astype(F32)).astype(BF).T

    order = [p.xs(2), p.xs(1), p.xs(-1), p.x]
    jobs = [{"sib": []} for _ in range(3)]

    def terms(j, blocks):
        for i in blocks:
            x = order[i]
            t = lax.dot_general(x2[:, rows_of(x * GW, GW, 128)], dproj[:, pl.ds(j * GW, GW)], TN,
                                preferred_element_type=F32).astype(BF)
            for c in range(2):
                for yh in range(2):
                    lo = (yh * 2 + c) * WROWS
                    part[j, i, c, yh] = t[lo:lo + WROWS]
            jobs[j]["sib"].append(net.go(part.at[j, i, 1 - p.c], sibl.at[j, i], sib))

    def add(j, i, yh, *lands):
        t = part[j, i, p.c, yh].astype(F32) + sibl[j, i, yh].astype(F32)
        for ref in lands:
            t = t + ref.astype(F32)
        return t

    def x_first(j):
        jobs[j]["sib"][0].wait_recv()
        for yh in range(2):
            other[j, 0, yh] = add(j, 0, yh).astype(BF)
        jobs[j]["a"] = net.go(other.at[j, 0, 0], land_a.at[j], right)
        jobs[j]["b"] = net.go(other.at[j, 0, 1], land_b.at[j], left)

    def x_second(j):
        job = jobs[j]
        job["sib"][1].wait_recv()
        job["sib"][2].wait_recv()
        other[j, 1, 1] = add(j, 1, 1).astype(BF)
        other[j, 2, 0] = add(j, 2, 0).astype(BF)
        job["a"].wait_recv()
        other[j, 1, 0] = add(j, 1, 0, land_a[j]).astype(BF)
        job["l"] = net.go(other.at[j, 1], land_l.at[j], right)
        job["b"].wait_recv()
        other[j, 2, 1] = add(j, 2, 1, land_b[j]).astype(BF)
        job["r"] = net.go(other.at[j, 2], land_r.at[j], left)

    def peer(yl, d, yh=None):
        return p.device(yh=yh, yl=yl, z=zs[d])

    def piece(z):
        return rows_of(z * 48, 48, 16)

    def dp_sum(j):
        job = jobs[j]
        job["sib"][3].wait_recv()
        job["l"].wait_recv()
        job["r"].wait_recv()
        for r in range(2):
            t = add(j, 3, r, land_l[j, r], land_r[j, r]).astype(BF)
            for i in range(3):
                zbuf[j, r, pl.ds(i * WROWS, WROWS), :] = t[:, i * 128:(i + 1) * 128]
        job["z"] = []
        for d in (4, 3, 5, 2, 6, 1, 7, 0):
            for a in ((0, 1) if d else (1,)):
                yl = p.yl if a == 0 else 1 - p.yl
                target = zs[d]
                cp = net.make(zbuf.at[j, lax.rem(p.yh + yl, 2), piece(lax.rem(target, 6))],
                              z_in.at[j, a * 8 + d], peer(yl, d))
                job["z"].append((cp, target, a * 8 + d))

                @pl.when(target < 6)
                def _(cp=cp):
                    cp.start()

    def dp_share(j):
        job = jobs[j]

        @pl.when(p.z < 6)
        def _():
            r = lax.rem(p.yh + p.yl, 2)
            t = zbuf[j, r, piece(p.z), :].astype(F32)
            for cp, _, slot in job["z"]:
                cp.wait_recv()
                t = t + z_in[j, slot].astype(F32)
            own[j] = t.astype(BF)

            @pl.when(p.yl == 0)
            def _():
                fin[j, 0, piece(p.z), :] = own[j]

        for cp, target, _ in job["z"]:
            @pl.when(target < 6)
            def _(cp=cp):
                cp.wait_send()

        job["f"] = []
        base = net.n
        net.n += 16
        for d in (4, 3, 5, 2, 6, 1, 7, 0):
            for yl in range(2):
                cp = pltpu.make_async_remote_copy(
                    src_ref=own.at[j], dst_ref=fin.at[j, p.yl, piece(lax.rem(p.z, 6))],
                    send_sem=send.at[base + yl * 8 + d], recv_sem=recv.at[base + p.yl * 8 + d],
                    device_id=peer(yl, d, lax.rem(p.yh + p.yl, 2)), device_id_type=MESH)
                source = lax.rem(p.z + (8 - d), 8)
                land = fin.at[j, yl, piece(lax.rem(source, 6))]
                arrive = pltpu.make_async_remote_copy(
                    src_ref=land, dst_ref=land, send_sem=send.at[base + yl * 8 + d],
                    recv_sem=recv.at[base + yl * 8 + d], device_id=right, device_id_type=MESH)
                real = p.z < 6
                comes = source < 6
                if d == 0 and yl == 0:
                    real = jnp.logical_and(real, p.yl == 1)
                    comes = jnp.logical_and(comes, p.yl == 1)
                job["f"].append((cp, real, arrive, comes))

                @pl.when(real)
                def _(cp=cp):
                    cp.start()

    def write(j):
        for cp, real, arrive, comes in jobs[j]["f"]:
            @pl.when(comes)
            def _(arrive=arrive):
                arrive.wait_recv()

            @pl.when(real)
            def _(cp=cp):
                cp.wait_send()

        for g in range(2):
            t = fin[j, lax.rem(p.yh + g, 2)]
            for i in range(3):
                gw[:, pl.ds(j * 2 * GW + g * GW + i * 128, 128)] = t[i * WROWS:(i + 1) * WROWS]

    def far(j):
        part_cols = pl.ds(j * GW, GW)
        return net.go(dproj.at[far_rows, part_cols], dfar.at[:, part_cols], ypair)

    fars = [far(0)]
    terms(0, (0,))
    terms(0, (1, 2, 3))
    x_first(0)
    for h in range(GROUP):
        own_k[h].wait_recv()
        lands[h].wait_recv()
        t = kpart[1, h, 1].astype(F32) + ksib[1, h].astype(F32) + kland[h].astype(F32)
        dproj[:, pl.ds(GW + h * HEAD, HEAD)] = t[:, :HEAD].astype(BF)
        dproj[:, pl.ds(2 * GW + h * HEAD, HEAD)] = t[:, HEAD:].astype(BF)
    fars += [far(1), far(2)]
    terms(1, (0,))
    terms(2, (0,))
    x_second(0)
    x_first(1)
    x_first(2)
    terms(1, (1, 2))
    terms(2, (1, 2))
    dp_sum(0)
    x_second(1)
    x_second(2)
    terms(1, (3,))
    terms(2, (3,))
    w_far.wait_recv()
    w_sib = net.go(w3.at[half_w], w3.at[half_w], sib)
    dp_share(0)
    dp_sum(1)
    dp_sum(2)
    dp_share(1)
    dp_share(2)
    part_gi = lax.dot_general(dproj[my_rows, :], w2[...], NT, preferred_element_type=F32)
    w_sib.wait_recv()
    for cp in fars:
        cp.wait_recv()
    gi[...] = (part_gi + lax.dot_general(dfar[...], w3[...], NT, preferred_element_type=F32)).astype(BF)
    write(0)
    write(1)
    write(2)
    al.wait()
    ao.wait_recv()
    net.drain()


def copy_kernel(att, gi, gw, att_out, gi_out, gw_out, a, b, c, sems):
    jobs = ((att, a, att_out.at[0]), (gi, b, gi_out.at[0]), (gw, c, gw_out))
    into = [pltpu.make_async_copy(src, mid, sems.at[i]) for i, (src, mid, _) in enumerate(jobs)]
    back = [pltpu.make_async_copy(mid, dst, sems.at[3 + i]) for i, (_, mid, dst) in enumerate(jobs)]
    for cp in into:
        cp.start()
    for x, y in zip(into, back):
        x.wait()
        y.start()
    for cp in back:
        cp.wait()


VMEM = pl.BlockSpec(memory_space=pltpu.VMEM)
ANY = pl.BlockSpec(memory_space=pl.ANY)


def on_device(seq_embed, w_qkv, upstream):
    scratch = [
        ((N, D), BF), ((D, GC), BF), ((2 * N, KW), BF), ((2, 2, N, KW), BF),
        ((8, 2 * N), F32), ((8, 2 * N), F32), ((GW, 2 * N), F32), ((16, 2 * N), F32), ((16, 2 * N), F32),
        ((8, 2 * N), F32), ((8, 2 * N), F32),
        ((GW, N), BF), ((GW, N), BF), ((N, GW), BF), ((GW, 2 * N), F32), ((GW, N), BF), ((GW, N), BF),
        ((2, GROUP, 2, N, 2 * HEAD), BF), ((GROUP, N, 2 * HEAD), BF), ((2, GROUP, N, 2 * HEAD), BF),
        ((GROUP, N, 2 * HEAD), BF), ((N, GC), BF),
        ((3, 4, 2, 2, WROWS, GW), BF), ((3, 3, 2, WROWS, GW), BF), ((3, 4, 2, WROWS, GW), BF),
        ((3, WROWS, GW), BF), ((3, WROWS, GW), BF), ((3, 2, WROWS, GW), BF), ((3, 2, WROWS, GW), BF),
        ((ROWS, GC), BF), ((D, GC), BF),
        ((3, 2, 288, 128), BF), ((3, 16, 48, 128), BF), ((3, 48, 128), BF), ((3, 2, 288, 128), BF),
    ]
    copies = 192
    att, gi, gw = pl.pallas_call(
        step_kernel,
        out_shape=[jax.ShapeDtypeStruct(s, BF) for s in ((ROWS, KW), (ROWS, D), (WROWS, 2 * GC))],
        in_specs=[ANY] * 3,
        out_specs=[VMEM] * 3,
        scratch_shapes=[pltpu.VMEM(s, t) for s, t in scratch] + [
            pltpu.SemaphoreType.DMA((copies,)), pltpu.SemaphoreType.DMA((copies,)),
            pltpu.SemaphoreType.DMA((8,))],
        compiler_params=pltpu.CompilerParams(
            collective_id=0, has_side_effects=True, vmem_limit_bytes=58 * 2**20),
    )(seq_embed[0], w_qkv, upstream[0])
    return pl.pallas_call(
        copy_kernel,
        out_shape=[jax.ShapeDtypeStruct(s, BF) for s in ((1, ROWS, KW), (1, ROWS, D), (WROWS, 2 * GC))],
        in_specs=[ANY] * 3,
        out_specs=[ANY] * 3,
        scratch_shapes=[pltpu.VMEM(s, BF) for s in ((ROWS, KW), (ROWS, D), (WROWS, 2 * GC))] + [
            pltpu.SemaphoreType.DMA((6,))],
    )(att, gi, gw)


def solution(mesh):
    placed = (P("dp", "seq", None), P("seq", None), P("dp", "seq", None))
    return jax.shard_map(
        on_device,
        mesh=mesh,
        in_specs=placed,
        out_specs=(P("dp", "seq", None), P("dp", "seq", None), P("seq", None)),
        check_vma=False,
    )
```
